768 devices in a mesh: task: 96 (over z, y), blk: 8 (over x, core).
Axes of the slice: x: 4, y: 8, z: 12, core: 2. Of those that a mesh axis runs over, the one named last changes fastest.
Arguments:
- coeffs: bfloat16 [6144, 96, 1024], P(('task', 'blk')), may hold values from -1.09375 to 1.09375
- coulomb: bfloat16 [3072, 9216], P(('task', 'blk')), may hold values from -0.625 to 0.625
- density: bfloat16 [512, 1024], P('blk'), may hold values from -6 to 6
- task_owner: int32 [49152, 1], P(('task', 'blk')), may hold values from 0 to 7; in each aligned block of 64 rows (0 to 63, 64 to 127, ...) at most 16 rows name the same one
- task_slot: int32 [49152], P(('task', 'blk')), may hold values from 0 to 63
- task_left: int32 [49152], P(('task', 'blk')), may hold values from 0 to 7
- task_right: int32 [49152], P(('task', 'blk')), may hold values from 0 to 7
- task_aux: int32 [49152], P(('task', 'blk')), may hold values from 0 to 3
- task_dest: int32 [49152], P(('task', 'blk')), may hold values from 0 to 767, as said below
Outputs:
- exchange_k: float32 [768, 1024], P(('task', 'blk'))
The draws below stay inside these ranges and needn't reach their ends.
Inputs may be any that keep to these rules, and one draw needn't show every extreme that they name: `task_owner`: among the tasks of one device no owner is named by more than 16 tasks, and some device reaches 16. Among the tasks of one device at most 16 have a task_dest with the same remainder modulo 8, and every device reaches 16 for some remainder.
All inputs are finite; a program needn't handle non-finite values.
Results may differ from the reference program's by a relative error of at most 0.0041.
Values may be sent and summed in bfloat16 or wider, within the bound.
No kernel may reach another device: no remote copies, remote signals or barrier semaphores. Data moves between devices by JAX's collectives and lax.ppermute only.
A program may use at most 32 MiB of HBM per device.

```python
import math
import jax
import jax.numpy as jnp
import numpy as np
from jax import lax

NO = 32
NA = 96
TASK_DEV = 64
CDEV = 8
VDEV = 4
DM_DEV = 64
DMCAP = 16
TASKS = 49152
CBLK = 6144
VBLK = 3072
NDM = 512
NK = 768
N_TASK = 96
N_BLK = 8


def draw_task_dest(key, part):
    key = jax.random.fold_in(key, 11)
    key_class, key_order, key_index = jax.random.split(key, 3)
    groups = TASKS // TASK_DEV
    base = jnp.arange(TASK_DEV, dtype=jnp.int32) % N_BLK
    heavy = jax.random.randint(key_class, (groups, 1), 0, N_BLK, dtype=jnp.int32)
    emptied = (heavy + 1) % N_BLK
    classes = jnp.where(base[None, :] == emptied, heavy, base[None, :])
    order = jax.vmap(lambda k: jax.random.permutation(k, TASK_DEV))(jax.random.split(key_order, groups))
    classes = jnp.take_along_axis(classes, order.astype(jnp.int32), axis=1)
    task_index = jax.random.randint(key_index, (groups, TASK_DEV), 0, N_TASK, dtype=jnp.int32)
    return (task_index * N_BLK + classes).reshape(TASKS).astype(jnp.int32)


def plant(array, rng, smallest, largest):
    dims = array.shape
    spot = [jax.random.randint(jax.random.fold_in(rng, axis), (), 0, dims[axis]) for axis in range(len(dims))]
    array = array.at[tuple(spot)].set(smallest)
    longest = dims.index(max(dims))
    spot[longest] = (spot[longest] + 1) % dims[longest]
    return array.at[tuple(spot)].set(largest)


def steps_of(stream_key, shape, cuts, smallest, largest):
    loudness = 1.0
    for dim, shards_of in cuts:
        steps = jax.random.uniform(jax.random.fold_in(jax.random.fold_in(stream_key, 6), dim), (shards_of,), jnp.float32, smallest / len(cuts), largest / len(cuts))
        loudness = loudness * jnp.repeat(jnp.exp(steps), shape[dim] // shards_of).reshape((-1,) + (1,) * (len(shape) - 1 - dim))
    return loudness


def deal_out(rng, own, number, rows, count, top, bound, slope):
    order = jax.random.permutation(rng, count)
    crowded, usual = portions_of(count, rows * top, bound, slope, True), portions_of(count, rows * top, bound, slope, False)
    places = jnp.arange(count)

    def named(tallies, rotation):
        used = int((tallies > 0).sum())
        fixed = max(1, used // 4)
        moved = fixed + (places - fixed + rotation * (used - fixed)) % max(1, count - fixed)
        return jnp.zeros((count,), jnp.int32).at[order[jnp.where(places < fixed, places, moved)]].set(jnp.asarray(tallies, jnp.int32))

    tallies = jnp.where(number % 4 == 0, named(crowded, number // 4), named(usual, number - number // 4 - 1))
    mixed = jax.random.permutation(jax.random.fold_in(own, 3), count)
    source_of, receiver = mixed[0:count // 2 * 2:2], mixed[1:count // 2 * 2:2]
    slack = jnp.minimum(tallies[source_of] - 1, bound - tallies[receiver]) // 2
    slack = jnp.where((source_of == order[0]) | (receiver == order[0]) | (tallies[receiver] == 0), 0, jnp.maximum(slack, 0))
    moved = jax.random.randint(jax.random.fold_in(own, 4), (count // 2,), 0, 1 << 20) % (slack + 1)
    tallies = tallies.at[source_of].add(-moved).at[receiver].add(moved)
    labels = jnp.searchsorted(jnp.cumsum(tallies), jnp.arange(rows * top), side="right").astype(jnp.int32)
    grid = labels.reshape(top, rows).T
    grid = grid[jax.random.permutation(jax.random.fold_in(own, 1), rows)]
    rotation = jax.random.randint(jax.random.fold_in(own, 2), (rows, 1), 0, top)
    return jnp.take_along_axis(grid, (jnp.arange(top)[None, :] + rotation) % top, axis=1)


def portions_of(amount, total, reach, slope, full):
    weights = [(1 << 20) // math.isqrt(grade ** slope) + 1 for grade in range(1, amount + 1)]
    largest = reach if full else min(reach, max(-(-total // amount), total * weights[0] // sum(weights)))
    least = 1 if total - largest >= amount - 1 else 0
    given, rest = [largest] + [least] * (amount - 1), total - largest - least * (amount - 1)
    while rest > 0:
        movable = [i for i in range(1, amount) if given[i] < largest] or [i for i in range(1, amount) if given[i] < reach]
        pool, remaining = sum([weights[i] for i in movable]), rest
        for i in movable:
            extra = min(reach - given[i], max(1, remaining * weights[i] // pool), rest)
            given[i] = given[i] + extra
            rest = rest - extra
    return np.array(given)


def noise(key, extent, deviation, bound, cuts=(), kind=jnp.bfloat16):
    gain = steps_of(key, extent, cuts, -0.22, 0.18) if cuts else 1.0
    entries = jax.random.normal(key, extent, jnp.float32) * deviation * gain
    return jnp.minimum(jnp.maximum(entries, -bound), bound).astype(kind)


def setup_inputs(seed: int = 0) -> dict:
    arg_keys = jax.random.split(jax.random.key(seed), 10)
    coeffs = noise(arg_keys[0], (CBLK, NA, NO * NO), 0.18, 1.09375, ((0, 768),))
    coulomb = noise(arg_keys[1], (VBLK, NA * NA), NA ** -0.5, 0.625, ((0, 768),))
    density = noise(arg_keys[2], (NDM, NO * NO), 1.0, 6.0, ((0, 8),))
    task_owner_keys = jax.random.split(jax.random.fold_in(arg_keys[3], 1), TASKS // TASK_DEV)
    task_owner_turns = jax.random.permutation(jax.random.fold_in(arg_keys[3], 3), TASKS // TASK_DEV)
    task_owner = jax.vmap(lambda own, number: deal_out(jax.random.fold_in(arg_keys[3], 2), own, number, TASK_DEV, N_BLK, 1, DMCAP, 2))(task_owner_keys, task_owner_turns).reshape((TASKS, 1))
    task_slot = plant(jax.random.randint(arg_keys[4], (TASKS,), 0, DM_DEV), jax.random.fold_in(arg_keys[4], 1), 0, DM_DEV - 1).astype(jnp.int32)
    task_left = plant(jax.random.randint(arg_keys[5], (TASKS,), 0, CDEV), jax.random.fold_in(arg_keys[5], 1), 0, CDEV - 1).astype(jnp.int32)
    task_right = plant(jax.random.randint(arg_keys[6], (TASKS,), 0, CDEV), jax.random.fold_in(arg_keys[6], 1), 0, CDEV - 1).astype(jnp.int32)
    task_aux = plant(jax.random.randint(arg_keys[7], (TASKS,), 0, VDEV), jax.random.fold_in(arg_keys[7], 1), 0, VDEV - 1).astype(jnp.int32)
    task_dest = draw_task_dest(jax.random.fold_in(arg_keys[9], 71), 0)
    return {"coeffs": coeffs, "coulomb": coulomb, "density": density, "task_owner": task_owner, "task_slot": task_slot, "task_left": task_left, "task_right": task_right, "task_aux": task_aux, "task_dest": task_dest}


def task_block(left_blocks, right_blocks, coulomb_blocks, density_blocks):
    left_full = left_blocks.astype(jnp.float32).reshape(-1, NA, NO, NO)
    right_full = right_blocks.astype(jnp.float32).reshape(-1, NA, NO, NO)
    density_full = density_blocks.astype(jnp.float32).reshape(-1, NO, NO)
    coulomb_full = coulomb_blocks.astype(jnp.float32).reshape(-1, NA, NA)
    contracted = jnp.einsum("tnjl,tkl->tnjk", right_full, density_full).astype(jnp.bfloat16)
    contracted = lax.optimization_barrier(contracted)
    applied = jnp.einsum("tmn,tnjk->tmjk", coulomb_full, contracted.astype(jnp.float32)).astype(jnp.bfloat16)
    applied = lax.optimization_barrier(applied)
    partial_k = jnp.einsum("tmik,tmjk->tij", left_full, applied.astype(jnp.float32))
    return partial_k.reshape(-1, NO * NO)


def reference(coeffs, coulomb, density, task_owner, task_slot, task_left, task_right, task_aux, task_dest):
    device_of = jnp.arange(TASKS, dtype=jnp.int32) // TASK_DEV
    left_index = (device_of * CDEV + task_left).astype(jnp.int32)
    right_index = (device_of * CDEV + task_right).astype(jnp.int32)
    aux_index = (device_of * VDEV + task_aux).astype(jnp.int32)
    density_index = (task_owner[:, 0] * DM_DEV + task_slot).astype(jnp.int32)
    groups = TASKS // TASK_DEV
    stacked = (left_index.reshape(groups, TASK_DEV), right_index.reshape(groups, TASK_DEV),
               aux_index.reshape(groups, TASK_DEV), density_index.reshape(groups, TASK_DEV),
               task_dest.reshape(groups, TASK_DEV))

    def one_group(total, pieces):
        left_rows, right_rows, aux_rows, density_rows, dest_rows = pieces
        partial_k = task_block(coeffs[left_rows], coeffs[right_rows], coulomb[aux_rows], density[density_rows])
        return total.at[dest_rows].add(partial_k), None

    start_total = jnp.zeros((NK, NO * NO), jnp.float32)
    total, unused = lax.scan(one_group, start_total, stacked)
    return -0.25 * total
```

```python
import functools
import jax
import jax.numpy as jnp
from jax import lax
from jax.experimental import pallas as pl
from jax.experimental.pallas import tpu as pltpu

BF = jnp.bfloat16
F32 = jnp.float32
VM = pl.BlockSpec(memory_space=pltpu.VMEM)
SM = pl.BlockSpec(memory_space=pltpu.SMEM)


def chunk_of():
    return lax.broadcasted_iota(jnp.int32, (8, 128), 1) // 32


def turn(y_ref, base):
    chunk = chunk_of()
    even = chunk % 2 == 0
    low = chunk < 2
    halves = []
    for h in range(2):
        x = [y_ref[pl.ds(base + 4 * h + m, 8, stride=8), :] for m in range(4)]
        y = [None] * 4
        for p in (0, 2):
            y[p] = jnp.where(even, x[p], pltpu.roll(x[p + 1], 32, 1))
            y[p + 1] = jnp.where(even, pltpu.roll(x[p], 96, 1), x[p + 1])
        z = [None] * 4
        for p in (0, 1):
            moved = pltpu.roll(jnp.where(low, y[p + 2], y[p]), 64, 1)
            z[p] = jnp.where(low, y[p], moved)
            z[p + 2] = jnp.where(low, moved, y[p + 2])
        halves.append(jnp.concatenate(z, axis=0))
    return jnp.concatenate(halves, axis=1).astype(BF)


def prepare(coeffs_ref, coulomb_ref, w_ref, l_ref, y_ref):
    blocks, na, cells = coeffs_ref.shape
    vrows = coulomb_ref.shape[0]
    aux = vrows // na
    tiles = na // 8

    def one(r, carry):
        vall = coulomb_ref[...]
        for q in range(cells // 256):
            right = coeffs_ref[r, :, q * 256:(q + 1) * 256]
            y = jnp.dot(vall, right, preferred_element_type=F32)
            full = jnp.concatenate([y, right.astype(F32)], axis=0)
            for e in range(2):
                v = 2 * q + e
                for mt in range((vrows + na) // 8):
                    y_ref[mt * 64 + v * 8:mt * 64 + v * 8 + 8, :] = full[mt * 8:mt * 8 + 8, e * 128:(e + 1) * 128]

        def one_tile(s, c):
            for a in range(aux):
                w_ref[r * aux + a, pl.ds(pl.multiple_of(s * 32, 32), 32), :] = turn(y_ref, (a * tiles + s) * 64)
            l_ref[s, pl.ds(pl.multiple_of(r * 32, 32), 32), :] = turn(y_ref, (aux * tiles + s) * 64)
            return c

        lax.fori_loop(0, tiles, one_tile, 0)
        return carry

    lax.fori_loop(0, blocks, one, 0)


def run_prepare(coeffs, vall):
    blocks, na, cells = coeffs.shape
    aux = vall.shape[0] // na
    tiles = na // 8
    return pl.pallas_call(
        prepare,
        out_shape=(
            jax.ShapeDtypeStruct((blocks * aux, tiles * 32, 256), BF),
            jax.ShapeDtypeStruct((tiles, blocks * 32, 256), BF),
        ),
        in_specs=[VM, VM],
        out_specs=(VM, VM),
        scratch_shapes=[pltpu.VMEM(((vall.shape[0] + na) * 8, 128), F32)],
        compiler_params=pltpu.CompilerParams(vmem_limit_bytes=48 * 2**20),
    )(coeffs, vall)


def tasks_kernel(me_ref, owner_ref, slot_ref, left_ref, right_ref, aux_ref, dest_ref, w_ref, l_ref, d_ref,
                 out_ref, a_ref, p_ref, count_ref):
    tasks = slot_ref.shape[0]
    peers, cap = out_ref.shape[0], out_ref.shape[1] - 1
    tiles = l_ref.shape[0]
    aux = w_ref.shape[0] // 8
    out_ref[...] = jnp.zeros_like(out_ref)
    for b in range(peers):
        count_ref[b] = 0

    row = lax.broadcasted_iota(jnp.int32, (256, 64), 0)
    col = lax.broadcasted_iota(jnp.int32, (256, 64), 1)
    spread = (row // 4 == col).astype(F32).astype(BF)
    krow = lax.broadcasted_iota(jnp.int32, (256, 128), 0)
    kchunk = lax.broadcasted_iota(jnp.int32, (256, 128), 1) // 32
    own_chunk = krow % 4 == kchunk
    pr = lax.broadcasted_iota(jnp.int32, (128, 256), 0)
    pc = lax.broadcasted_iota(jnp.int32, (128, 256), 1)
    repeat = (pr % 32 == pc % 32).astype(F32).astype(BF)
    br = lax.broadcasted_iota(jnp.int32, (256, 256), 0)
    bc = lax.broadcasted_iota(jnp.int32, (256, 256), 1)
    diag = (br // 32 == bc // 32).astype(F32).astype(BF)
    chunk = chunk_of()
    lane = lax.broadcasted_iota(jnp.int32, (8, 128), 1)
    me = me_ref[0]

    def group(g, carry):
        base = g * 8
        picked = [d_ref[owner_ref[base + t] * 64 + slot_ref[base + t]].astype(F32) for t in range(8)]
        stacked = jnp.concatenate(picked, axis=0).astype(BF)
        e = jnp.dot(spread, stacked, preferred_element_type=F32)
        e = jnp.where(own_chunk, e, 0.0).astype(BF)
        dl = jnp.dot(e, repeat, preferred_element_type=F32).astype(BF)
        for t in range(8):
            bd = jnp.concatenate([dl[t * 32:(t + 1) * 32]] * 8, axis=0) * diag
            w = w_ref[right_ref[base + t] * aux + aux_ref[base + t]]
            y = lax.dot_general(w, bd, (((1,), (1,)), ((), ())), preferred_element_type=F32).astype(BF)
            for s in range(tiles):
                a_ref[t * 32:(t + 1) * 32, s * 256:(s + 1) * 256] = y[s * 32:(s + 1) * 32, :]
        total = jnp.zeros((256, 256), F32)
        for s in range(tiles):
            total += lax.dot_general(l_ref[s], a_ref[:, s * 256:(s + 1) * 256], (((1,), (1,)), ((), ())), preferred_element_type=F32)
        p_ref[...] = total
        for t in range(8):
            top = left_ref[base + t] * 32
            half, mine = t // 4, t % 4
            block = None
            for q in range(4):
                piece = p_ref[pl.ds(pl.multiple_of(top + q * 8, 8), 8), half * 128:(half + 1) * 128]
                if q != mine:
                    piece = pltpu.roll(piece, ((q - mine) * 32) % 128, 1)
                block = piece if block is None else jnp.where(chunk == q, piece, block)
            dest = dest_ref[base + t]
            peer = lax.rem(dest, peers)
            place = count_ref[peer]
            count_ref[peer] = place + 1
            out_ref[peer, place] = block
            name = (dest // peers + 1).astype(F32)
            out_ref[peer, cap] = jnp.where(lane == me * cap + place, name, out_ref[peer, cap])
        return carry

    lax.fori_loop(0, tasks // 8, group, 0)


def run_tasks(me, owner, slot, left, right, aux, dest, w, l, dens, peers, cap):
    return pl.pallas_call(
        tasks_kernel,
        out_shape=jax.ShapeDtypeStruct((peers, cap + 1, 8, 128), F32),
        in_specs=[SM] * 7 + [VM] * 3,
        out_specs=VM,
        scratch_shapes=[
            pltpu.VMEM((256, l.shape[0] * 256), BF),
            pltpu.VMEM((256, 256), F32),
            pltpu.SMEM((peers,), jnp.int32),
        ],
        compiler_params=pltpu.CompilerParams(vmem_limit_bytes=48 * 2**20),
    )(me, owner, slot, left, right, aux, dest, w, l, dens)


def spread_kernel(recv_ref, out_ref, flat_ref):
    peers, slots = recv_ref.shape[0], recv_ref.shape[1]
    cap = slots - 1
    rows = out_ref.shape[0]
    names = recv_ref[0, cap]
    for p in range(1, peers):
        names = names + recv_ref[p, cap]
    wanted = lax.broadcasted_iota(jnp.int32, (rows, 128), 0) + 1
    hot = (wanted == jnp.broadcast_to(names[0:1, :], (rows, 128)).astype(jnp.int32)).astype(F32).astype(BF)
    for p in range(peers):
        for n in range(cap):
            flat_ref[(p * cap + n) * 8:(p * cap + n + 1) * 8, :] = recv_ref[p, n]
    sums = []
    for i in range(8):
        x = flat_ref[pl.ds(i, 128, stride=8), :]
        hi = x.astype(BF)
        lo = (x - hi.astype(F32)).astype(BF)
        both = jnp.dot(hot, hi, preferred_element_type=F32) + jnp.dot(hot, lo, preferred_element_type=F32)
        flat2 = both
        sums.append(flat2)
    for i in range(8):
        flat_ref[pl.ds(i, rows, stride=8), :] = sums[i]
    out_ref[...] = flat_ref[0:rows * 8, :].reshape(rows, 8, 128).astype(out_ref.dtype)


def run_spread(recv, rows, dtype):
    peers, slots = recv.shape[:2]
    return pl.pallas_call(
        spread_kernel,
        out_shape=jax.ShapeDtypeStruct((rows, 8, 128), dtype),
        in_specs=[VM],
        out_specs=VM,
        scratch_shapes=[pltpu.VMEM((max(rows, peers * (slots - 1)) * 8, 128), F32)],
        compiler_params=pltpu.CompilerParams(vmem_limit_bytes=32 * 2**20),
    )(recv)


def final_kernel(recv_ref, out_ref):
    rows = recv_ref.shape[0]
    total = jnp.sum(recv_ref[...].astype(F32), axis=0) * -0.25
    r = lax.broadcasted_iota(jnp.int32, (128, 128), 0)
    c = lax.broadcasted_iota(jnp.int32, (128, 128), 1)
    source = (c // 32) * 32 + (c % 4) * 8 + (c % 32) // 4
    move = (r == source).astype(F32)
    out_ref[...] = jnp.dot(total, move, preferred_element_type=F32, precision=lax.Precision.HIGHEST)


def run_final(recv):
    return pl.pallas_call(
        final_kernel,
        out_shape=jax.ShapeDtypeStruct((8, 128), F32),
        in_specs=[VM],
        out_specs=VM,
    )(recv)
def per_device(coeffs, coulomb, density, task_owner, task_slot, task_left, task_right, task_aux, task_dest):
    na = coeffs.shape[1]
    blk, task = lax.axis_size("blk"), lax.axis_size("task")
    w, l = run_prepare(coeffs, coulomb.reshape(coulomb.shape[0] * na, na))
    mine = density.reshape(density.shape[0], 8, 128)
    dens = lax.all_to_all(jnp.broadcast_to(mine, (blk, *mine.shape)), "blk", 0, 0, tiled=True)
    dens = dens.reshape(blk * mine.shape[0], 8, 128)
    me = lax.axis_index("blk").astype(jnp.int32).reshape(1)
    send = run_tasks(me, task_owner.reshape(-1), task_slot, task_left, task_right, task_aux, task_dest, w, l, dens, blk, 16)
    recv = lax.all_to_all(send, "blk", 0, 0, tiled=True)
    rows = run_spread(recv, task, BF)
    back = lax.all_to_all(rows, "task", 0, 0, tiled=True)
    return run_final(back).reshape(1, 1024)


def solution(mesh):
    from jax.sharding import PartitionSpec as P
    both = P(("task", "blk"))
    placed = (P(("task", "blk"), None, None), P(("task", "blk"), None), P("blk", None), P(("task", "blk"), None), both, both, both, both, both)
    return jax.shard_map(per_device, mesh=mesh, in_specs=placed, out_specs=P(("task", "blk"), None), check_vma=False)
```

```python
import jax
import jax.numpy as jnp
from jax import lax
from jax.experimental import pallas as pl
from jax.experimental.pallas import tpu as pltpu
from jax.sharding import PartitionSpec as P

BF = jnp.bfloat16
F32 = jnp.float32
MB = 2**20
VM = pl.BlockSpec(memory_space=pltpu.VMEM)
SM = pl.BlockSpec(memory_space=pltpu.SMEM)
HB = pl.BlockSpec(memory_space=pltpu.HBM)
PEERS = 8
CORES = 2
HELD = 64


def iota(shape, dim):
    return lax.broadcasted_iota(jnp.int32, shape, dim)


def ones_where(mask):
    return jnp.where(mask, 1.0, 0.0).astype(BF)


def pack_kernel(d_ref, out_ref, flat_ref):
    blocks, cells = d_ref.shape
    d = d_ref[...]
    for b in range(cells // 256):
        col = iota((256, 256), 1) + b * 256
        source = (col % 32) * 32 + col // 32
        y = jnp.zeros((blocks, 256), F32)
        for a in range(cells // 256):
            move = ones_where(iota((256, 256), 0) + a * 256 == source)
            y += jnp.dot(d[:, a * 256:(a + 1) * 256], move, preferred_element_type=F32)
        for e in range(2):
            flat_ref[pl.ds(2 * b + e, blocks, stride=8), :] = y[:, e * 128:(e + 1) * 128]
    x = flat_ref[...].reshape(blocks, 8, 128).astype(BF)
    for p in range(out_ref.shape[0]):
        out_ref[p] = x


def run_pack(density, peers):
    blocks = density.shape[0]
    return pl.pallas_call(
        pack_kernel,
        out_shape=jax.ShapeDtypeStruct((peers, blocks, 8, 128), BF),
        in_specs=[VM],
        out_specs=VM,
        scratch_shapes=[pltpu.VMEM((blocks * 8, 128), F32)],
        compiler_params=pltpu.CompilerParams(vmem_limit_bytes=8 * MB),
    )(density)


def turned(x_ref, move_ref, top, tiles):
    z = jnp.dot(x_ref[top:top + tiles * 16, :], move_ref[...], preferred_element_type=F32)
    blocks = []
    for s in range(tiles):
        halves = []
        for h in range(2):
            row = (s * 2 + h) * 8
            halves.append(jnp.concatenate([z[row:row + 8, c * 128:(c + 1) * 128] for c in range(4)], axis=0))
        blocks.append(jnp.concatenate(halves, axis=1).astype(BF))
    return blocks


def prepare(me_ref, owner_ref, slot_ref, left_ref, right_ref, aux_ref, dest_ref, coeffs_ref, coulomb_ref,
            w_out, l_out, table_ref, names_ref, count_ref, y_ref, x_ref, move_ref, lw_ref, l_ref, w_ref, w_sem, l_sem):
    blocks, na, cells = coeffs_ref.shape
    vrows = coulomb_ref.shape[0]
    aux = vrows // na
    tiles = na // 8
    tasks = slot_ref.shape[0]
    share = tasks // blocks
    peers, cap = PEERS, 128 // PEERS
    sub, lane = iota((8, 128), 0), iota((8, 128), 1)
    me = me_ref[0]
    for b in range(blocks + peers):
        count_ref[b] = 0

    def count_some(r):
        for u in range(share):
            right = right_ref[r * share + u]
            count_ref[right] = count_ref[right] + 1

    def place_some(r, names):
        for u in range(share):
            t = r * share + u
            right = right_ref[t]
            spot = count_ref[right]
            count_ref[right] = spot + 1
            dest = dest_ref[t]
            peer = lax.rem(dest, peers)
            place = count_ref[blocks + peer]
            count_ref[blocks + peer] = place + 1
            owner = owner_ref[t]
            table_ref[spot] = lax.rem(owner, CORES) * (HELD * peers // CORES) + owner // CORES * HELD + slot_ref[t]
            table_ref[tasks + spot] = right * aux + aux_ref[t]
            table_ref[2 * tasks + spot] = left_ref[t]
            table_ref[3 * tasks + spot] = peer * (cap + 1) + place
            table_ref[4 * tasks + spot] = right
            name = (dest // peers + 1).astype(F32)
            names = jnp.where((sub == peer) & (lane == me * cap + place), name, names)
        return names

    row, col = iota((512, 512), 0), iota((512, 512), 1)
    move_ref[...] = ones_where(row == (col % 128) // 32 * 128 + col // 128 * 32 + col % 32)

    def store(full, q, count):
        for e in range(2):
            v = 2 * q + e
            for mt in range(count):
                y_ref[mt * 64 + v * 8:mt * 64 + v * 8 + 8, :] = full[mt * 8:mt * 8 + 8, e * 128:(e + 1) * 128]

    def gather(count):
        for mt in range(count):
            for m in range(4):
                pair = [y_ref[pl.ds(mt * 64 + 4 * h + m, 8, stride=8), :] for h in range(2)]
                x_ref[mt * 16:(mt + 1) * 16, m * 128:(m + 1) * 128] = jnp.concatenate(pair, axis=0).astype(BF)

    def one_left(r, carry):
        for q in range(cells // 256):
            store(coeffs_ref[r, :, q * 256:(q + 1) * 256].astype(F32), q, tiles)
        gather(tiles)
        for s, block in enumerate(turned(x_ref, move_ref, 0, tiles)):
            lw_ref[s, pl.ds(pl.multiple_of(r * 32, 32), 32), :] = block
        count_some(r)
        return carry

    lax.fori_loop(0, blocks, one_left, 0, unroll=4)
    first = 0
    for r in range(blocks):
        many = count_ref[r]
        count_ref[r] = first
        first = first + many
    for s in range(tiles):
        l_ref[s * 256:(s + 1) * 256, :] = jnp.transpose(lw_ref[s])
    l_copy = pltpu.make_async_copy(l_ref, l_out, l_sem)
    l_copy.start()

    def w_copy(r):
        part = pl.ds(r * aux, aux)
        return pltpu.make_async_copy(w_ref.at[part], w_out.at[part], w_sem.at[r])

    def one(r, names):
        vall = coulomb_ref[...]
        for q in range(cells // 256):
            store(jnp.dot(vall, coeffs_ref[r, :, q * 256:(q + 1) * 256], preferred_element_type=F32), q, aux * tiles)
        gather(aux * tiles)
        for a in range(aux):
            for s, block in enumerate(turned(x_ref, move_ref, a * tiles * 16, tiles)):
                w_ref[r * aux + a, s * 32:(s + 1) * 32, :] = block
        w_copy(r).start()
        return place_some(r, names)

    names_ref[...] = lax.fori_loop(0, blocks, one, jnp.zeros((8, 128), F32), unroll=2)
    for r in range(blocks):
        w_copy(r).wait()
    l_copy.wait()


def run_prepare(me, owner, slot, left, right, aux_of, dest, coeffs, vall):
    blocks, na, cells = coeffs.shape
    aux = vall.shape[0] // na
    tiles = na // 8
    rows = vall.shape[0] + na
    return pl.pallas_call(
        prepare,
        out_shape=(
            pltpu.HBM((blocks * aux, tiles * 32, 256), BF),
            pltpu.HBM((tiles * 256, blocks * 32), BF),
            jax.ShapeDtypeStruct((1024,), jnp.int32),
            jax.ShapeDtypeStruct((8, 128), F32),
        ),
        in_specs=[SM] * 7 + [VM, VM],
        out_specs=(HB, HB, SM, VM),
        scratch_shapes=[
            pltpu.SMEM((blocks + PEERS,), jnp.int32),
            pltpu.VMEM((rows * 8, 128), F32),
            pltpu.VMEM((rows * 2, 512), BF),
            pltpu.VMEM((512, 512), BF),
            pltpu.VMEM((tiles, blocks * 32, 256), BF),
            pltpu.VMEM((tiles * 256, blocks * 32), BF),
            pltpu.VMEM((blocks * aux, tiles * 32, 256), BF),
            pltpu.SemaphoreType.DMA((blocks,)),
            pltpu.SemaphoreType.DMA,
        ],
        compiler_params=pltpu.CompilerParams(vmem_limit_bytes=24 * MB),
    )(me, owner, slot, left, right, aux_of, dest, coeffs, vall)


def tasks_kernel(table_ref, names_ref, w_in, l_in, d_ref,
                 out_ref, dl_ref, a0_ref, a1_ref, send_ref, w_ref, l_ref, w_sem, l_sem):
    tiles = l_ref.shape[0] // 256
    lefts = l_ref.shape[1] // 32
    aux = w_ref.shape[0] // lefts
    tasks = dl_ref.shape[0] // 32
    groups = tasks // 8
    slots = out_ref.shape[1]

    def w_copy(r):
        part = pl.ds(r * aux, aux)
        return pltpu.make_async_copy(w_in.at[part], w_ref.at[part], w_sem.at[r])

    l_copy = pltpu.make_async_copy(l_in, l_ref, l_sem)
    w_copy(0).start()
    l_copy.start()
    for r in range(1, lefts):
        w_copy(r).start()
    send_ref[...] = jnp.zeros_like(send_ref)

    spread = ones_where(iota((256, 64), 0) // 4 == iota((256, 64), 1))
    own_chunk = iota((256, 128), 0) % 4 == iota((256, 128), 1) // 32
    repeat = ones_where(iota((128, 256), 0) % 32 == iota((128, 256), 1) % 32)
    for g in range(groups):
        picked = [d_ref[table_ref[g * 8 + u]].astype(F32) for u in range(8)]
        e = jnp.dot(spread, jnp.concatenate(picked, axis=0).astype(BF), preferred_element_type=F32)
        e = jnp.where(own_chunk, e, 0.0).astype(BF)
        dl_ref[g * 256:(g + 1) * 256, :] = jnp.dot(e, repeat, preferred_element_type=F32).astype(BF)

    diag = ones_where(iota((256, 256), 0) // 32 == iota((256, 256), 1) // 32)
    fold = ones_where(iota((256, 128), 0) % 32 == iota((256, 128), 1) % 32)
    chunk = iota((8, 128), 1) // 32
    column = iota((32, 256), 1) // 32

    def apply(g, a_ref):
        for u in range(8):
            d = dl_ref[pl.ds(pl.multiple_of(g * 256 + u * 32, 32), 32), :]
            bd = jnp.concatenate([d] * 8, axis=0) * diag
            w = w_ref[table_ref[tasks + g * 8 + u]]
            y = jnp.dot(w, bd, preferred_element_type=F32).astype(BF)
            for s in range(tiles):
                a_ref[u * 32:(u + 1) * 32, s * 256:(s + 1) * 256] = y[s * 32:(s + 1) * 32, :]

    def close(g, a_ref):
        total = jnp.dot(a_ref[...], l_ref[...], preferred_element_type=F32)
        own = [jnp.where(column == table_ref[2 * tasks + g * 8 + u], total[u * 32:(u + 1) * 32, :], 0.0) for u in range(8)]
        total = jnp.dot(jnp.concatenate(own, axis=0).astype(BF), fold, preferred_element_type=F32)
        for u in range(8):
            block = total[u * 32:u * 32 + 8, :]
            for q in range(1, 4):
                block = jnp.where(chunk == q, total[u * 32 + q * 8:u * 32 + q * 8 + 8, :], block)
            send_ref[table_ref[3 * tasks + g * 8 + u]] = block

    def wait_to(g, waited):
        last = table_ref[4 * tasks + g * 8 + 7] + 1

        def wait(r, c):
            w_copy(r).wait()
            return c

        lax.fori_loop(waited, last, wait, 0)
        return jnp.maximum(waited, last)

    waited = wait_to(0, jnp.int32(0))
    apply(0, a0_ref)
    l_copy.wait()

    def two(h, waited):
        waited = wait_to(2 * h + 2, waited)
        apply(2 * h + 1, a1_ref)
        close(2 * h, a0_ref)
        apply(2 * h + 2, a0_ref)
        close(2 * h + 1, a1_ref)
        return waited

    waited = lax.fori_loop(0, groups // 2 - 1, two, waited)
    waited = wait_to(groups - 1, waited)
    apply(groups - 1, a1_ref)
    close(groups - 2, a0_ref)
    close(groups - 1, a1_ref)

    def drain(r, c):
        w_copy(r).wait()
        return c

    lax.fori_loop(waited, lefts, drain, 0)
    names = names_ref[...]
    for p in range(out_ref.shape[0]):
        send_ref[p * slots + slots - 1] = jnp.broadcast_to(names[p:p + 1, :], (8, 128))
    out_ref[...] = send_ref[...].reshape(out_ref.shape).astype(out_ref.dtype)


def run_tasks(table, names, w, l, dens, tasks, peers, cap):
    w = pltpu.with_memory_space_constraint(w, pltpu.HBM)
    l = pltpu.with_memory_space_constraint(l, pltpu.HBM)
    return pl.pallas_call(
        tasks_kernel,
        out_shape=jax.ShapeDtypeStruct((peers, cap + 1, 8, 128), BF),
        in_specs=[SM, VM, HB, HB, VM],
        out_specs=VM,
        scratch_shapes=[
            pltpu.VMEM((tasks * 32, 256), BF),
            pltpu.VMEM((256, l.shape[0]), BF),
            pltpu.VMEM((256, l.shape[0]), BF),
            pltpu.VMEM((peers * (cap + 1), 8, 128), F32),
            pltpu.VMEM(w.shape, BF),
            pltpu.VMEM(l.shape, BF),
            pltpu.SemaphoreType.DMA((l.shape[1] // 32,)),
            pltpu.SemaphoreType.DMA,
        ],
        compiler_params=pltpu.CompilerParams(vmem_limit_bytes=24 * MB),
    )(table, names, w, l, dens)


def spread_kernel(recv_ref, out_ref, flat_ref):
    peers, slots = recv_ref.shape[0], recv_ref.shape[1]
    cap = slots - 1
    rows = out_ref.shape[0]
    names = recv_ref[0, cap].astype(F32)
    for p in range(1, peers):
        names = names + recv_ref[p, cap].astype(F32)
    names = jnp.broadcast_to(names[0:1, :], (rows, 128)).astype(jnp.int32)
    hot = ones_where(iota((rows, 128), 0) + 1 == names)
    for p in range(peers):
        for n in range(cap):
            flat_ref[(p * cap + n) * 8:(p * cap + n + 1) * 8, :] = recv_ref[p, n].astype(F32)
    sums = []
    for i in range(8):
        x = flat_ref[pl.ds(i, 128, stride=8), :]
        sums.append(jnp.dot(hot, x.astype(BF), preferred_element_type=F32))
    for i in range(8):
        flat_ref[pl.ds(i, rows, stride=8), :] = sums[i]
    out_ref[...] = flat_ref[0:rows * 8, :].reshape(rows, 8, 128).astype(out_ref.dtype)


def run_spread(recv, rows, dtype):
    peers, slots = recv.shape[:2]
    return pl.pallas_call(
        spread_kernel,
        out_shape=jax.ShapeDtypeStruct((rows, 8, 128), dtype),
        in_specs=[VM],
        out_specs=VM,
        scratch_shapes=[pltpu.VMEM((max(rows, peers * (slots - 1)) * 8, 128), F32)],
        compiler_params=pltpu.CompilerParams(vmem_limit_bytes=8 * MB),
    )(recv)


def exact_dot(x, y):
    out = None
    for _ in range(3):
        part = x.astype(BF)
        x = x - part.astype(F32)
        term = jnp.dot(part, y, preferred_element_type=F32)
        out = term if out is None else out + term
    return out


def final_kernel(recv_ref, out_ref):
    total = jnp.sum(recv_ref[...].astype(F32), axis=0) * -0.25
    vi = iota((64, 128), 0) // 8
    wide = jnp.concatenate([total] * 8, axis=0)
    wide = jnp.where(iota((64, 128), 1) % 8 == vi, wide, 0.0)
    r, c = iota((128, 128), 0), iota((128, 128), 1)
    move = ones_where((r // 32 == c % 4) & (r % 32 // 8 == c // 32))
    wide = exact_dot(wide, move)
    wide = jnp.where(iota((64, 128), 1) % 32 // 4 == iota((64, 128), 0) % 8, wide, 0.0)
    out_ref[...] = jnp.sum(wide.reshape(8, 8, 128), axis=1)


def run_final(recv):
    return pl.pallas_call(
        final_kernel,
        out_shape=jax.ShapeDtypeStruct((8, 128), F32),
        in_specs=[VM],
        out_specs=VM,
        compiler_params=pltpu.CompilerParams(vmem_limit_bytes=4 * MB),
    )(recv)


def per_device(coeffs, coulomb, density, task_owner, task_slot, task_left, task_right, task_aux, task_dest):
    na = coeffs.shape[1]
    blk, task = lax.axis_size("blk"), lax.axis_size("task")
    chips = blk // CORES
    same_core = [[x * CORES + c for x in range(chips)] for c in range(CORES)]
    same_chip = [[x * CORES + c for c in range(CORES)] for x in range(chips)]
    dens = lax.all_to_all(run_pack(density, chips), "blk", 0, 0, tiled=True, axis_index_groups=same_core)
    me = lax.axis_index("blk").astype(jnp.int32).reshape(1)
    w, l, table, names = run_prepare(me, task_owner.reshape(-1), task_slot, task_left, task_right, task_aux, task_dest,
                                     coeffs, coulomb.reshape(coulomb.shape[0] * na, na))
    dens = lax.all_gather(dens.reshape(chips * HELD, 8, 128), "blk", axis=0, tiled=True, axis_index_groups=same_chip)
    send = run_tasks(table, names, w, l, dens, task_slot.shape[0], blk, 128 // blk)
    recv = lax.all_to_all(send, "blk", 0, 0, tiled=True)
    rows = run_spread(recv, task, BF)
    back = lax.all_to_all(rows, "task", 0, 0, tiled=True)
    return run_final(back).reshape(1, density.shape[1])


def solution(mesh):
    every = P(("task", "blk"))
    placed = (every, every, P("blk"), every, every, every, every, every, every)
    return jax.shard_map(per_device, mesh=mesh, in_specs=placed, out_specs=every, check_vma=False)
```

```python
import jax
import jax.numpy as jnp
from jax import lax
from jax.experimental import pallas as pl
from jax.experimental.pallas import tpu as pltpu
from jax.sharding import PartitionSpec as P

BF = jnp.bfloat16
F32 = jnp.float32
MB = 2**20
VM = pl.BlockSpec(memory_space=pltpu.VMEM)
SM = pl.BlockSpec(memory_space=pltpu.SMEM)
HB = pl.BlockSpec(memory_space=pltpu.HBM)
PEERS = 8
CORES = 2
HELD = 64
AUX = 4


def iota(shape, dim):
    return lax.broadcasted_iota(jnp.int32, shape, dim)


def ones_where(mask):
    return jnp.where(mask, 1.0, 0.0).astype(BF)


def pack_kernel(d_ref, out_ref, flat_ref):
    blocks, cells = d_ref.shape
    d = d_ref[...]
    for b in range(cells // 256):
        col = iota((256, 256), 1) + b * 256
        source = (col % 32) * 32 + col // 32
        y = jnp.zeros((blocks, 256), F32)
        for a in range(cells // 256):
            move = ones_where(iota((256, 256), 0) + a * 256 == source)
            y += jnp.dot(d[:, a * 256:(a + 1) * 256], move, preferred_element_type=F32)
        for e in range(2):
            flat_ref[pl.ds(2 * b + e, blocks, stride=8), :] = y[:, e * 128:(e + 1) * 128]
    x = flat_ref[...].reshape(blocks, 8, 128).astype(BF)
    for p in range(out_ref.shape[0]):
        out_ref[p] = x


def run_pack(density, peers):
    blocks = density.shape[0]
    return pl.pallas_call(
        pack_kernel,
        out_shape=jax.ShapeDtypeStruct((peers, blocks, 8, 128), BF),
        in_specs=[VM],
        out_specs=VM,
        scratch_shapes=[pltpu.VMEM((blocks * 8, 128), F32)],
        compiler_params=pltpu.CompilerParams(vmem_limit_bytes=8 * MB),
    )(density)


def lane_move():
    row, col = iota((512, 512), 0), iota((512, 512), 1)
    return ones_where(row == (col % 128) // 32 * 128 + col // 128 * 32 + col % 32)


def put_rows(y_ref, full, q, count):
    for e in range(2):
        v = 2 * q + e
        for mt in range(count):
            y_ref[mt * 64 + v * 8:mt * 64 + v * 8 + 8, :] = full[mt * 8:mt * 8 + 8, e * 128:(e + 1) * 128]


def gather_rows(y_ref, x_ref, first, count):
    for mt in range(first, first + count):
        for m in range(4):
            pair = [y_ref[pl.ds(mt * 64 + 4 * h + m, 8, stride=8), :] for h in range(2)]
            x_ref[mt * 16:(mt + 1) * 16, m * 128:(m + 1) * 128] = jnp.concatenate(pair, axis=0).astype(BF)


def turned(x_ref, move_ref, first, tiles):
    z = jnp.dot(x_ref[first * 16:(first + tiles) * 16, :], move_ref[...], preferred_element_type=F32)
    blocks = []
    for s in range(tiles):
        halves = []
        for h in range(2):
            row = (s * 2 + h) * 8
            halves.append(jnp.concatenate([z[row:row + 8, c * 128:(c + 1) * 128] for c in range(4)], axis=0))
        blocks.append(jnp.concatenate(halves, axis=1).astype(BF))
    return blocks


def lefts_kernel(me_ref, owner_ref, slot_ref, left_ref, right_ref, aux_ref, dest_ref, coeffs_ref,
                 l_out, table_ref, names_ref, count_ref, y0_ref, y1_ref, x0_ref, x1_ref, move_ref, lw_ref, l_ref, l_sem):
    blocks, na, cells = coeffs_ref.shape
    tiles = na // 8
    tasks = slot_ref.shape[0]
    share = tasks // blocks
    peers, cap = PEERS, 128 // PEERS
    sub, lane = iota((8, 128), 0), iota((8, 128), 1)
    me = me_ref[0]
    for b in range(blocks + peers):
        count_ref[b] = 0
    move_ref[...] = lane_move()

    def count_some(r):
        for u in range(share):
            right = right_ref[r * share + u]
            count_ref[right] = count_ref[right] + 1

    def place_some(r, names):
        for u in range(share):
            t = r * share + u
            right = right_ref[t]
            spot = count_ref[right]
            count_ref[right] = spot + 1
            dest = dest_ref[t]
            peer = lax.rem(dest, peers)
            place = count_ref[blocks + peer]
            count_ref[blocks + peer] = place + 1
            owner = owner_ref[t]
            table_ref[spot] = lax.rem(owner + me, CORES) * (HELD * peers // CORES) + owner // CORES * HELD + slot_ref[t]
            table_ref[tasks + spot] = right * AUX + aux_ref[t]
            table_ref[2 * tasks + spot] = left_ref[t]
            table_ref[3 * tasks + spot] = peer * (cap + 1) + place
            table_ref[4 * tasks + spot] = right
            name = (dest // peers + 1).astype(F32)
            names = jnp.where((sub == peer) & (lane == me * cap + place), name, names)
        return names

    for r in range(blocks):
        count_some(r)
    first = 0
    for r in range(blocks):
        many = count_ref[r]
        count_ref[r] = first
        first = first + many

    def two(h, names):
        for e, (y_ref, x_ref) in enumerate(((y0_ref, x0_ref), (y1_ref, x1_ref))):
            r = 2 * h + e
            for q in range(cells // 256):
                put_rows(y_ref, coeffs_ref[r, :, q * 256:(q + 1) * 256].astype(F32), q, tiles)
            gather_rows(y_ref, x_ref, 0, tiles)
            for s, block in enumerate(turned(x_ref, move_ref, 0, tiles)):
                lw_ref[s, pl.ds(pl.multiple_of(r * 32, 32), 32), :] = block
            names = place_some(r, names)
        return names

    names_ref[...] = lax.fori_loop(0, blocks // 2, two, jnp.zeros((8, 128), F32), unroll=2)
    for s in range(tiles):
        l_ref[s * 256:(s + 1) * 256, :] = jnp.transpose(lw_ref[s])
    l_copy = pltpu.make_async_copy(l_ref, l_out, l_sem)
    l_copy.start()
    l_copy.wait()


def run_lefts(me, owner, slot, left, right, aux_of, dest, coeffs):
    blocks, na, cells = coeffs.shape
    tiles = na // 8
    return pl.pallas_call(
        lefts_kernel,
        out_shape=(
            pltpu.HBM((tiles * 256, blocks * 32), BF),
            jax.ShapeDtypeStruct((1024,), jnp.int32),
            jax.ShapeDtypeStruct((8, 128), F32),
        ),
        in_specs=[SM] * 7 + [VM],
        out_specs=(HB, SM, VM),
        scratch_shapes=[
            pltpu.SMEM((blocks + PEERS,), jnp.int32),
            pltpu.VMEM((na * 8, 128), F32),
            pltpu.VMEM((na * 8, 128), F32),
            pltpu.VMEM((na * 2, 512), BF),
            pltpu.VMEM((na * 2, 512), BF),
            pltpu.VMEM((512, 512), BF),
            pltpu.VMEM((tiles, blocks * 32, 256), BF),
            pltpu.VMEM((tiles * 256, blocks * 32), BF),
            pltpu.SemaphoreType.DMA,
        ],
        compiler_params=pltpu.CompilerParams(vmem_limit_bytes=16 * MB),
    )(me, owner, slot, left, right, aux_of, dest, coeffs)


def rights_kernel(coeffs_ref, coulomb_ref, after_ref, w_out, y0_ref, y1_ref, x0_ref, x1_ref, move_ref, w_ref, w_sem):
    blocks, na, cells = coeffs_ref.shape
    vrows = coulomb_ref.shape[0]
    aux = vrows // na
    tiles = na // 8
    move_ref[...] = lane_move()

    def w_copy(r):
        part = pl.ds(r * aux, aux)
        return pltpu.make_async_copy(w_ref.at[part], w_out.at[part], w_sem.at[r])

    def multiply(r, y_ref):
        for q in range(cells // 256):
            y = jnp.dot(coulomb_ref[...], coeffs_ref[r, :, q * 256:(q + 1) * 256], preferred_element_type=F32)
            put_rows(y_ref, y, q, aux * tiles)

    def turn(r, y_ref, x_ref):
        for a in range(aux):
            gather_rows(y_ref, x_ref, a * tiles, tiles)
            for s, block in enumerate(turned(x_ref, move_ref, a * tiles, tiles)):
                w_ref[r * aux + a, s * 32:(s + 1) * 32, :] = block
        w_copy(r).start()

    multiply(0, y0_ref)

    def two(h, carry):
        multiply(2 * h + 1, y1_ref)
        turn(2 * h, y0_ref, x0_ref)
        multiply(jnp.minimum(2 * h + 2, blocks - 1), y0_ref)
        turn(2 * h + 1, y1_ref, x1_ref)
        return carry

    lax.fori_loop(0, blocks // 2, two, 0)
    for r in range(blocks):
        w_copy(r).wait()


def run_rights(coeffs, vall, after):
    blocks, na, cells = coeffs.shape
    aux = vall.shape[0] // na
    tiles = na // 8
    rows = vall.shape[0]
    return pl.pallas_call(
        rights_kernel,
        out_shape=pltpu.HBM((blocks * aux, tiles * 32, 256), BF),
        in_specs=[VM, VM, pl.BlockSpec(memory_space=pl.ANY)],
        out_specs=HB,
        scratch_shapes=[
            pltpu.VMEM((rows * 8, 128), F32),
            pltpu.VMEM((rows * 8, 128), F32),
            pltpu.VMEM((rows * 2, 512), BF),
            pltpu.VMEM((rows * 2, 512), BF),
            pltpu.VMEM((512, 512), BF),
            pltpu.VMEM((blocks * aux, tiles * 32, 256), BF),
            pltpu.SemaphoreType.DMA((blocks,)),
        ],
        compiler_params=pltpu.CompilerParams(vmem_limit_bytes=24 * MB),
    )(coeffs, vall, after)


def tasks_kernel(table_ref, names_ref, w_in, l_in, d_ref, e_ref,
                 out_ref, dl_ref, a0_ref, a1_ref, send_ref, w_ref, l_ref, w_sem, l_sem):
    tiles = l_ref.shape[0] // 256
    lefts = l_ref.shape[1] // 32
    aux = w_ref.shape[0] // lefts
    tasks = dl_ref.shape[0] // 32
    groups = tasks // 8
    slots = out_ref.shape[1]
    half = d_ref.shape[0]

    def w_copy(r):
        part = pl.ds(r * aux, aux)
        return pltpu.make_async_copy(w_in.at[part], w_ref.at[part], w_sem.at[r])

    l_copy = pltpu.make_async_copy(l_in, l_ref, l_sem)
    w_copy(0).start()
    l_copy.start()
    for r in range(1, lefts):
        w_copy(r).start()
    send_ref[...] = jnp.zeros_like(send_ref)

    spread = ones_where(iota((256, 64), 0) // 4 == iota((256, 64), 1))
    own_chunk = iota((256, 128), 0) % 4 == iota((256, 128), 1) // 32
    repeat = ones_where(iota((128, 256), 0) % 32 == iota((128, 256), 1) % 32)
    for g in range(groups):
        picked = []
        for u in range(8):
            spot = table_ref[g * 8 + u]
            here = lax.rem(spot, half)
            picked.append(jnp.where(spot < half, d_ref[here].astype(F32), e_ref[here].astype(F32)))
        e = jnp.dot(spread, jnp.concatenate(picked, axis=0).astype(BF), preferred_element_type=F32)
        e = jnp.where(own_chunk, e, 0.0).astype(BF)
        dl_ref[g * 256:(g + 1) * 256, :] = jnp.dot(e, repeat, preferred_element_type=F32).astype(BF)

    diag = ones_where(iota((256, 256), 0) // 32 == iota((256, 256), 1) // 32)
    fold = ones_where(iota((256, 128), 0) % 32 == iota((256, 128), 1) % 32)
    chunk = iota((8, 128), 1) // 32
    column = iota((32, 256), 1) // 32

    def apply(g, a_ref):
        for u in range(8):
            d = dl_ref[pl.ds(pl.multiple_of(g * 256 + u * 32, 32), 32), :]
            bd = jnp.concatenate([d] * 8, axis=0) * diag
            w = w_ref[table_ref[tasks + g * 8 + u]]
            y = jnp.dot(w, bd, preferred_element_type=F32).astype(BF)
            for s in range(tiles):
                a_ref[u * 32:(u + 1) * 32, s * 256:(s + 1) * 256] = y[s * 32:(s + 1) * 32, :]

    def close(g, a_ref):
        total = jnp.dot(a_ref[...], l_ref[...], preferred_element_type=F32)
        own = [jnp.where(column == table_ref[2 * tasks + g * 8 + u], total[u * 32:(u + 1) * 32, :], 0.0) for u in range(8)]
        total = jnp.dot(jnp.concatenate(own, axis=0).astype(BF), fold, preferred_element_type=F32)
        for u in range(8):
            block = total[u * 32:u * 32 + 8, :]
            for q in range(1, 4):
                block = jnp.where(chunk == q, total[u * 32 + q * 8:u * 32 + q * 8 + 8, :], block)
            send_ref[table_ref[3 * tasks + g * 8 + u]] = block

    def wait_to(g, waited):
        last = table_ref[4 * tasks + g * 8 + 7] + 1

        def wait(r, c):
            w_copy(r).wait()
            return c

        lax.fori_loop(waited, last, wait, 0)
        return jnp.maximum(waited, last)

    waited = wait_to(0, jnp.int32(0))
    apply(0, a0_ref)
    l_copy.wait()

    def two(h, waited):
        waited = wait_to(2 * h + 2, waited)
        apply(2 * h + 1, a1_ref)
        close(2 * h, a0_ref)
        apply(2 * h + 2, a0_ref)
        close(2 * h + 1, a1_ref)
        return waited

    waited = lax.fori_loop(0, groups // 2 - 1, two, waited)
    waited = wait_to(groups - 1, waited)
    apply(groups - 1, a1_ref)
    close(groups - 2, a0_ref)
    close(groups - 1, a1_ref)

    def drain(r, c):
        w_copy(r).wait()
        return c

    lax.fori_loop(waited, lefts, drain, 0)
    names = names_ref[...]
    for p in range(out_ref.shape[0]):
        send_ref[p * slots + slots - 1] = jnp.broadcast_to(names[p:p + 1, :], (8, 128))
    out_ref[...] = send_ref[...].reshape(out_ref.shape).astype(out_ref.dtype)


def run_tasks(table, names, w, l, dens, other, tasks, peers, cap):
    w = pltpu.with_memory_space_constraint(w, pltpu.HBM)
    l = pltpu.with_memory_space_constraint(l, pltpu.HBM)
    return pl.pallas_call(
        tasks_kernel,
        out_shape=jax.ShapeDtypeStruct((peers, cap + 1, 8, 128), BF),
        in_specs=[SM, VM, HB, HB, VM, VM],
        out_specs=VM,
        scratch_shapes=[
            pltpu.VMEM((tasks * 32, 256), BF),
            pltpu.VMEM((256, l.shape[0]), BF),
            pltpu.VMEM((256, l.shape[0]), BF),
            pltpu.VMEM((peers * (cap + 1), 8, 128), F32),
            pltpu.VMEM(w.shape, BF),
            pltpu.VMEM(l.shape, BF),
            pltpu.SemaphoreType.DMA((l.shape[1] // 32,)),
            pltpu.SemaphoreType.DMA,
        ],
        compiler_params=pltpu.CompilerParams(vmem_limit_bytes=24 * MB),
    )(table, names, w, l, dens, other)


def spread_kernel(recv_ref, out_ref, flat_ref):
    peers, slots = recv_ref.shape[0], recv_ref.shape[1]
    cap = slots - 1
    rows = out_ref.shape[0]
    names = recv_ref[0, cap].astype(F32)
    for p in range(1, peers):
        names = names + recv_ref[p, cap].astype(F32)
    names = jnp.broadcast_to(names[0:1, :], (rows, 128)).astype(jnp.int32)
    hot = ones_where(iota((rows, 128), 0) + 1 == names)
    for p in range(peers):
        for n in range(cap):
            flat_ref[(p * cap + n) * 8:(p * cap + n + 1) * 8, :] = recv_ref[p, n].astype(F32)
    sums = []
    for i in range(8):
        x = flat_ref[pl.ds(i, 128, stride=8), :]
        sums.append(jnp.dot(hot, x.astype(BF), preferred_element_type=F32))
    for i in range(8):
        flat_ref[pl.ds(i, rows, stride=8), :] = sums[i]
    out_ref[...] = flat_ref[0:rows * 8, :].reshape(rows, 8, 128).astype(out_ref.dtype)


def run_spread(recv, rows, dtype):
    peers, slots = recv.shape[:2]
    return pl.pallas_call(
        spread_kernel,
        out_shape=jax.ShapeDtypeStruct((rows, 8, 128), dtype),
        in_specs=[VM],
        out_specs=VM,
        scratch_shapes=[pltpu.VMEM((max(rows, peers * (slots - 1)) * 8, 128), F32)],
        compiler_params=pltpu.CompilerParams(vmem_limit_bytes=8 * MB),
    )(recv)


def exact_dot(x, y):
    out = None
    for _ in range(3):
        part = x.astype(BF)
        x = x - part.astype(F32)
        term = jnp.dot(part, y, preferred_element_type=F32)
        out = term if out is None else out + term
    return out


def final_kernel(recv_ref, out_ref):
    total = jnp.sum(recv_ref[...].astype(F32), axis=0) * -0.25
    vi = iota((64, 128), 0) // 8
    wide = jnp.concatenate([total] * 8, axis=0)
    wide = jnp.where(iota((64, 128), 1) % 8 == vi, wide, 0.0)
    r, c = iota((128, 128), 0), iota((128, 128), 1)
    move = ones_where((r // 32 == c % 4) & (r % 32 // 8 == c // 32))
    wide = exact_dot(wide, move)
    wide = jnp.where(iota((64, 128), 1) % 32 // 4 == iota((64, 128), 0) % 8, wide, 0.0)
    out_ref[...] = jnp.sum(wide.reshape(8, 8, 128), axis=1)


def run_final(recv):
    return pl.pallas_call(
        final_kernel,
        out_shape=jax.ShapeDtypeStruct((8, 128), F32),
        in_specs=[VM],
        out_specs=VM,
        compiler_params=pltpu.CompilerParams(vmem_limit_bytes=4 * MB),
    )(recv)


def per_device(coeffs, coulomb, density, task_owner, task_slot, task_left, task_right, task_aux, task_dest):
    na = coeffs.shape[1]
    blk, task = lax.axis_size("x") * lax.axis_size("core"), lax.axis_size("task")
    chips = blk // CORES
    dens = lax.all_to_all(run_pack(density, chips), "x", 0, 0, tiled=True)
    me = lax.axis_index(BLK).astype(jnp.int32).reshape(1)
    l, table, names = run_lefts(me, task_owner.reshape(-1), task_slot, task_left, task_right, task_aux, task_dest, coeffs)
    dens = dens.reshape(chips * HELD, 8, 128)
    dens, l, table, names = lax.optimization_barrier((dens, l, table, names))
    other = lax.ppermute(dens, "core", [(0, 1), (1, 0)])
    w = run_rights(coeffs, coulomb.reshape(coulomb.shape[0] * na, na), dens)
    send = run_tasks(table, names, w, l, dens, other, task_slot.shape[0], blk, 128 // blk)
    recv = lax.all_to_all(send, BLK, 0, 0, tiled=True)
    rows = run_spread(recv, task, BF)
    back = lax.all_to_all(rows, "task", 0, 0, tiled=True)
    return run_final(back).reshape(1, density.shape[1])


BLK = ("x", "core")


def solution(mesh):
    sizes = (mesh.shape["task"], mesh.shape["blk"] // CORES, CORES)
    fine = jax.sharding.Mesh(mesh.devices.reshape(sizes), ("task", "x", "core"))
    every = P(("task", "x", "core"))
    placed = (every, every, P(BLK), every, every, every, every, every, every)
    return jax.shard_map(per_device, mesh=fine, in_specs=placed, out_specs=every, check_vma=False)
```

```python
import functools

import jax
import jax.numpy as jnp
from jax import lax
from jax.experimental import pallas as pl
from jax.experimental.pallas import tpu as pltpu
from jax.sharding import PartitionSpec as P

BF = jnp.bfloat16
F32 = jnp.float32
MB = 2**20
VM = pl.BlockSpec(memory_space=pltpu.VMEM)
SM = pl.BlockSpec(memory_space=pltpu.SMEM)
HB = pl.BlockSpec(memory_space=pltpu.HBM)
PEERS = 8
CORES = 2
HELD = 64
AUX = 4
CUT1, CUT2 = 3, 6


def iota(shape, dim):
    return lax.broadcasted_iota(jnp.int32, shape, dim)


def ones_where(mask):
    return jnp.where(mask, 1.0, 0.0).astype(BF)


def pack_kernel(d_ref, out_ref, flat_ref):
    blocks, cells = d_ref.shape
    d = d_ref[...]
    for b in range(cells // 256):
        col = iota((1, 256), 1) + b * 256
        source = ((col & 31) << 5) + (col >> 5)
        y = jnp.zeros((blocks, 256), F32)
        for a in range(cells // 256):
            move = ones_where(iota((256, 256), 0) == source - a * 256)
            y += jnp.dot(d[:, a * 256:(a + 1) * 256], move, preferred_element_type=F32)
        for e in range(2):
            flat_ref[pl.ds(2 * b + e, blocks, stride=8), :] = y[:, e * 128:(e + 1) * 128]
    x = flat_ref[...].reshape(blocks, 8, 128).astype(BF)
    for p in range(out_ref.shape[0]):
        out_ref[p] = x


def run_pack(density, peers):
    blocks = density.shape[0]
    return pl.pallas_call(
        pack_kernel,
        out_shape=jax.ShapeDtypeStruct((peers, blocks, 8, 128), BF),
        in_specs=[VM],
        out_specs=VM,
        scratch_shapes=[pltpu.VMEM((blocks * 8, 128), F32)],
        compiler_params=pltpu.CompilerParams(vmem_limit_bytes=8 * MB),
    )(density)


def lane_move():
    col = iota((1, 512), 1)
    source = ((col & 96) << 2) + ((col >> 7) << 5) + (col & 31)
    return ones_where(iota((512, 512), 0) == source)


def put_rows(y_ref, full, q, count):
    for e in range(2):
        v = 2 * q + e
        for mt in range(count):
            y_ref[mt * 64 + v * 8:mt * 64 + v * 8 + 8, :] = full[mt * 8:mt * 8 + 8, e * 128:(e + 1) * 128]


def gather_rows(y_ref, x_ref, first, count):
    for mt in range(first, first + count):
        for m in range(4):
            pair = [y_ref[pl.ds(mt * 64 + 4 * h + m, 8, stride=8), :] for h in range(2)]
            x_ref[mt * 16:(mt + 1) * 16, m * 128:(m + 1) * 128] = jnp.concatenate(pair, axis=0).astype(BF)


def turned(x_ref, move_ref, first, tiles):
    z = jnp.dot(x_ref[first * 16:(first + tiles) * 16, :], move_ref[...], preferred_element_type=F32)
    blocks = []
    for s in range(tiles):
        halves = []
        for h in range(2):
            row = (s * 2 + h) * 8
            halves.append(jnp.concatenate([z[row:row + 8, c * 128:(c + 1) * 128] for c in range(4)], axis=0))
        blocks.append(jnp.concatenate(halves, axis=1).astype(BF))
    return blocks


def lefts_kernel(me_ref, owner_ref, slot_ref, left_ref, right_ref, aux_ref, dest_ref, coeffs_ref,
                 l_out, table_ref, names_ref, count_ref, y0_ref, y1_ref, x0_ref, x1_ref, move_ref, lw_ref, l_ref, l_sem):
    blocks, na, cells = coeffs_ref.shape
    tiles = na // 8
    tasks = slot_ref.shape[0]
    share = tasks // blocks
    peers, cap = PEERS, 128 // PEERS
    sub, lane = iota((8, 128), 0), iota((8, 128), 1)
    me = me_ref[0]
    for b in range(peers):
        count_ref[b] = 0
    move_ref[...] = lane_move()

    def place_some(r, names):
        for u in range(share):
            t = r * share + u
            dest = dest_ref[t]
            peer = lax.rem(dest, peers)
            place = count_ref[peer]
            count_ref[peer] = place + 1
            owner = owner_ref[t]
            table_ref[t] = lax.rem(owner + me, CORES) * (HELD * peers // CORES) + owner // CORES * HELD + slot_ref[t]
            table_ref[tasks + t] = right_ref[t] * AUX + aux_ref[t]
            table_ref[2 * tasks + t] = left_ref[t]
            table_ref[3 * tasks + t] = peer * (cap + 1) + place
            name = (dest // peers + 1).astype(F32)
            names = jnp.where((sub == peer) & (lane == me * cap + place), name, names)
        return names

    def two(h, names):
        for e, (y_ref, x_ref) in enumerate(((y0_ref, x0_ref), (y1_ref, x1_ref))):
            r = 2 * h + e
            for q in range(cells // 256):
                put_rows(y_ref, coeffs_ref[r, :, q * 256:(q + 1) * 256].astype(F32), q, tiles)
            gather_rows(y_ref, x_ref, 0, tiles)
            for s, block in enumerate(turned(x_ref, move_ref, 0, tiles)):
                lw_ref[s, pl.ds(pl.multiple_of(r * 32, 32), 32), :] = block
            names = place_some(r, names)
        return names

    names_ref[...] = lax.fori_loop(0, blocks // 2, two, jnp.zeros((8, 128), F32), unroll=4)
    copies = []
    for s in range(tiles):
        part = pl.ds(s * 256, 256)
        l_ref[part, :] = jnp.transpose(lw_ref[s])
        copies.append(pltpu.make_async_copy(l_ref.at[part], l_out.at[part], l_sem.at[s]))
        copies[s].start()
    for copy in copies:
        copy.wait()


def run_lefts(me, owner, slot, left, right, aux_of, dest, coeffs):
    blocks, na, cells = coeffs.shape
    tiles = na // 8
    return pl.pallas_call(
        lefts_kernel,
        out_shape=(
            pltpu.HBM((tiles * 256, blocks * 32), BF),
            jax.ShapeDtypeStruct((1024,), jnp.int32),
            jax.ShapeDtypeStruct((8, 128), F32),
        ),
        in_specs=[SM] * 7 + [VM],
        out_specs=(HB, SM, VM),
        scratch_shapes=[
            pltpu.SMEM((PEERS,), jnp.int32),
            pltpu.VMEM((na * 8, 128), F32),
            pltpu.VMEM((na * 8, 128), F32),
            pltpu.VMEM((na * 2, 512), BF),
            pltpu.VMEM((na * 2, 512), BF),
            pltpu.VMEM((512, 512), BF),
            pltpu.VMEM((tiles, blocks * 32, 256), BF),
            pltpu.VMEM((tiles * 256, blocks * 32), BF),
            pltpu.SemaphoreType.DMA((tiles,)),
        ],
        compiler_params=pltpu.CompilerParams(vmem_limit_bytes=16 * MB),
    )(me, owner, slot, left, right, aux_of, dest, coeffs)


def multiply(coeffs_ref, coulomb_ref, r, y_ref):
    cells = coeffs_ref.shape[2]
    count = coulomb_ref.shape[0] // 8
    for q in range(cells // 256):
        y = jnp.dot(coulomb_ref[...], coeffs_ref[r, :, q * 256:(q + 1) * 256], preferred_element_type=F32)
        put_rows(y_ref, y, q, count)


def turn(y_ref, x_ref, move_ref, w_ref, first, tiles):
    for a in range(y_ref.shape[0] // (64 * tiles)):
        gather_rows(y_ref, x_ref, a * tiles, tiles)
        for s, block in enumerate(turned(x_ref, move_ref, a * tiles, tiles)):
            w_ref[first + a, s * 32:(s + 1) * 32, :] = block


def rights_kernel(begin, end, coeffs_ref, coulomb_ref, after_ref, w_out, y0_ref, y1_ref, x0_ref, x1_ref, move_ref, w_ref, w_sem):
    na = coeffs_ref.shape[1]
    aux = coulomb_ref.shape[0] // na
    tiles = na // 8
    move_ref[...] = lane_move()
    ys, xs = (y0_ref, y1_ref), (x0_ref, x1_ref)
    copies = []
    multiply(coeffs_ref, coulomb_ref, begin, ys[0])
    for r in range(begin, end):
        e = (r - begin) % 2
        if r + 1 < end:
            multiply(coeffs_ref, coulomb_ref, r + 1, ys[1 - e])
        turn(ys[e], xs[e], move_ref, w_ref, (r - begin) * aux, tiles)
        part = pl.ds((r - begin) * aux, aux)
        copies.append(pltpu.make_async_copy(w_ref.at[part], w_out.at[part], w_sem.at[r - begin]))
        copies[-1].start()
    for copy in copies:
        copy.wait()


def rights_scratch(rows):
    return [
        pltpu.VMEM((rows * 8, 128), F32),
        pltpu.VMEM((rows * 8, 128), F32),
        pltpu.VMEM((rows * 2, 512), BF),
        pltpu.VMEM((rows * 2, 512), BF),
        pltpu.VMEM((512, 512), BF),
    ]


def run_rights(coeffs, vall, after, begin, end):
    na = coeffs.shape[1]
    aux = vall.shape[0] // na
    shape = ((end - begin) * aux, na // 8 * 32, 256)
    return pl.pallas_call(
        functools.partial(rights_kernel, begin, end),
        out_shape=pltpu.HBM(shape, BF),
        in_specs=[VM, VM, pl.BlockSpec(memory_space=pl.ANY)],
        out_specs=HB,
        scratch_shapes=rights_scratch(vall.shape[0]) + [
            pltpu.VMEM(shape, BF),
            pltpu.SemaphoreType.DMA((end - begin,)),
        ],
        compiler_params=pltpu.CompilerParams(vmem_limit_bytes=20 * MB),
    )(coeffs, vall, after)


def tasks_kernel(table_ref, names_ref, coeffs_ref, coulomb_ref, w1_in, w2_in, l_in, d_ref, e_ref,
                 out_ref, y0_ref, y1_ref, x0_ref, x1_ref, move_ref, dl_ref, a_ref, send_ref, w_ref, l_ref, sem):
    tiles = l_ref.shape[0] // 256
    blocks = l_ref.shape[1] // 32
    aux = w_ref.shape[0] // blocks
    tasks = dl_ref.shape[0] // 32
    groups = tasks // 8
    slots = out_ref.shape[1]
    half = d_ref.shape[0]

    here = pl.ds(0, w1_in.shape[0])
    there = pl.ds(w1_in.shape[0], w2_in.shape[0])
    copies = [
        pltpu.make_async_copy(l_in, l_ref, sem.at[0]),
        pltpu.make_async_copy(w1_in, w_ref.at[here], sem.at[1]),
        pltpu.make_async_copy(w2_in, w_ref.at[there], sem.at[2]),
    ]
    for i in (1, 2, 0):
        copies[i].start()
    move_ref[...] = lane_move()
    ys, xs = (y0_ref, y1_ref), (x0_ref, x1_ref)
    begin = (w1_in.shape[0] + w2_in.shape[0]) // aux
    for r in range(begin, blocks):
        multiply(coeffs_ref, coulomb_ref, r, ys[r % 2])
    for r in range(begin, blocks):
        turn(ys[r % 2], xs[r % 2], move_ref, w_ref, r * aux, tiles)
    send_ref[...] = jnp.zeros_like(send_ref)

    spread = ones_where((iota((256, 64), 0) >> 2) == iota((256, 64), 1))
    own_chunk = (iota((256, 128), 0) & 3) == (iota((256, 128), 1) >> 5)
    repeat = ones_where((iota((128, 256), 0) & 31) == (iota((128, 256), 1) & 31))
    for g in range(groups):
        picked = []
        for u in range(8):
            spot = table_ref[g * 8 + u]
            here = lax.rem(spot, half)
            picked.append(jnp.where(spot < half, d_ref[here].astype(F32), e_ref[here].astype(F32)))
        e = jnp.dot(spread, jnp.concatenate(picked, axis=0).astype(BF), preferred_element_type=F32)
        e = jnp.where(own_chunk, e, 0.0).astype(BF)
        dl_ref[g * 256:(g + 1) * 256, :] = jnp.dot(e, repeat, preferred_element_type=F32).astype(BF)

    diag = ones_where((iota((256, 256), 0) >> 5) == (iota((256, 256), 1) >> 5))
    fold = ones_where((iota((256, 128), 0) & 31) == (iota((256, 128), 1) & 31))
    chunk = iota((8, 128), 1) >> 5
    column = iota((32, 256), 1) >> 5

    def apply(g, carry):
        for u in range(64):
            t = g * 64 + u
            rows = pl.ds(pl.multiple_of(t * 32, 32), 32)
            bd = jnp.concatenate([dl_ref[rows, :]] * 8, axis=0) * diag
            y = jnp.dot(w_ref[table_ref[tasks + t]], bd, preferred_element_type=F32).astype(BF)
            for s in range(tiles):
                a_ref[rows, s * 256:(s + 1) * 256] = y[s * 32:(s + 1) * 32, :]
        return carry

    def close(g, carry):
        rows = pl.ds(pl.multiple_of(g * 2048, 2048), 2048)
        total = jnp.dot(a_ref[rows, :], l_ref[...], preferred_element_type=F32)
        own = [jnp.where(column == table_ref[2 * tasks + g * 64 + u], total[u * 32:(u + 1) * 32, :], 0.0) for u in range(64)]
        total = jnp.dot(jnp.concatenate(own, axis=0).astype(BF), fold, preferred_element_type=F32)
        for u in range(64):
            block = total[u * 32:u * 32 + 8, :]
            for q in range(1, 4):
                block = jnp.where(chunk == q, total[u * 32 + q * 8:u * 32 + q * 8 + 8, :], block)
            send_ref[table_ref[3 * tasks + g * 64 + u]] = block
        return carry

    copies[1].wait()
    copies[2].wait()
    lax.fori_loop(0, tasks // 64, apply, 0)
    copies[0].wait()
    lax.fori_loop(0, tasks // 64, close, 0)
    names = names_ref[...]
    for p in range(out_ref.shape[0]):
        send_ref[p * slots + slots - 1] = jnp.broadcast_to(names[p:p + 1, :], (8, 128))
    out_ref[...] = send_ref[...].reshape(out_ref.shape).astype(out_ref.dtype)


def run_tasks(table, names, coeffs, vall, w1, w2, l, dens, other, tasks, peers, cap):
    w1, w2, l = (pltpu.with_memory_space_constraint(x, pltpu.HBM) for x in (w1, w2, l))
    blocks, na, _ = coeffs.shape
    return pl.pallas_call(
        tasks_kernel,
        out_shape=jax.ShapeDtypeStruct((peers, cap + 1, 8, 128), BF),
        in_specs=[SM, VM, VM, VM, HB, HB, HB, VM, VM],
        out_specs=VM,
        scratch_shapes=rights_scratch(vall.shape[0]) + [
            pltpu.VMEM((tasks * 32, 256), BF),
            pltpu.VMEM((tasks * 32, l.shape[0]), BF),
            pltpu.VMEM((peers * (cap + 1), 8, 128), F32),
            pltpu.VMEM((blocks * (vall.shape[0] // na),) + w1.shape[1:], BF),
            pltpu.VMEM(l.shape, BF),
            pltpu.SemaphoreType.DMA((3,)),
        ],
        compiler_params=pltpu.CompilerParams(vmem_limit_bytes=40 * MB),
    )(table, names, coeffs, vall, w1, w2, l, dens, other)


def spread_kernel(recv_ref, out_ref, flat_ref):
    peers, slots = recv_ref.shape[0], recv_ref.shape[1]
    cap = slots - 1
    rows = out_ref.shape[0]
    names = recv_ref[0, cap].astype(F32)
    for p in range(1, peers):
        names = names + recv_ref[p, cap].astype(F32)
    names = jnp.broadcast_to(names[0:1, :], (rows, 128)).astype(jnp.int32)
    hot = ones_where(iota((rows, 128), 0) + 1 == names)
    for p in range(peers):
        for n in range(cap):
            flat_ref[(p * cap + n) * 8:(p * cap + n + 1) * 8, :] = recv_ref[p, n].astype(F32)
    sums = []
    for i in range(8):
        x = flat_ref[pl.ds(i, 128, stride=8), :]
        sums.append(jnp.dot(hot, x.astype(BF), preferred_element_type=F32))
    for i in range(8):
        flat_ref[pl.ds(i, rows, stride=8), :] = sums[i]
    out_ref[...] = flat_ref[0:rows * 8, :].reshape(rows, 8, 128).astype(out_ref.dtype)


def run_spread(recv, rows, dtype):
    peers, slots = recv.shape[:2]
    return pl.pallas_call(
        spread_kernel,
        out_shape=jax.ShapeDtypeStruct((rows, 8, 128), dtype),
        in_specs=[VM],
        out_specs=VM,
        scratch_shapes=[pltpu.VMEM((max(rows, peers * (slots - 1)) * 8, 128), F32)],
        compiler_params=pltpu.CompilerParams(vmem_limit_bytes=8 * MB),
    )(recv)


def exact_dot(x, y):
    out = None
    for _ in range(3):
        part = x.astype(BF)
        x = x - part.astype(F32)
        term = jnp.dot(part, y, preferred_element_type=F32)
        out = term if out is None else out + term
    return out


def final_kernel(recv_ref, out_ref):
    total = jnp.sum(recv_ref[...].astype(F32), axis=0) * -0.25
    vi = iota((64, 128), 0) >> 3
    wide = jnp.concatenate([total] * 8, axis=0)
    wide = jnp.where((iota((64, 128), 1) & 7) == vi, wide, 0.0)
    r, c = iota((128, 128), 0), iota((128, 128), 1)
    move = ones_where((r >> 3) == ((c & 3) << 2) + (c >> 5))
    wide = exact_dot(wide, move)
    wide = jnp.where(((iota((64, 128), 1) >> 2) & 7) == (iota((64, 128), 0) & 7), wide, 0.0)
    out_ref[...] = jnp.sum(wide.reshape(8, 8, 128), axis=1)


def run_final(recv):
    return pl.pallas_call(
        final_kernel,
        out_shape=jax.ShapeDtypeStruct((8, 128), F32),
        in_specs=[VM],
        out_specs=VM,
        compiler_params=pltpu.CompilerParams(vmem_limit_bytes=4 * MB),
    )(recv)


def per_device(coeffs, coulomb, density, task_owner, task_slot, task_left, task_right, task_aux, task_dest):
    na = coeffs.shape[1]
    blk, task = lax.axis_size("x") * lax.axis_size("core"), lax.axis_size("task")
    chips = blk // CORES
    dens = lax.all_to_all(run_pack(density, chips), "x", 0, 0, tiled=True)
    me = lax.axis_index(BLK).astype(jnp.int32).reshape(1)
    vall = coulomb.reshape(coulomb.shape[0] * na, na)
    l, table, names = run_lefts(me, task_owner.reshape(-1), task_slot, task_left, task_right, task_aux, task_dest, coeffs)
    w1 = run_rights(coeffs, vall, names, 0, CUT1)
    dens = dens.reshape(chips * HELD, 8, 128)
    dens, l, table, names, w1 = lax.optimization_barrier((dens, l, table, names, w1))
    other = lax.ppermute(dens, "core", [(0, 1), (1, 0)])
    w2 = run_rights(coeffs, vall, dens, CUT1, CUT2)
    send = run_tasks(table, names, coeffs, vall, w1, w2, l, dens, other, task_slot.shape[0], blk, 128 // blk)
    recv = lax.all_to_all(send, BLK, 0, 0, tiled=True)
    rows = run_spread(recv, task, BF)
    back = lax.all_to_all(rows, "task", 0, 0, tiled=True)
    return run_final(back).reshape(1, density.shape[1])


BLK = ("x", "core")


def solution(mesh):
    sizes = (mesh.shape["task"], mesh.shape["blk"] // CORES, CORES)
    fine = jax.sharding.Mesh(mesh.devices.reshape(sizes), ("task", "x", "core"))
    every = P(("task", "x", "core"))
    placed = (every, every, P(BLK), every, every, every, every, every, every)
    return jax.shard_map(per_device, mesh=fine, in_specs=placed, out_specs=every, check_vma=False)
```

```python
import functools

import jax
import jax.numpy as jnp
from jax import lax
from jax.experimental import pallas as pl
from jax.experimental.pallas import tpu as pltpu
from jax.sharding import PartitionSpec as P

BF = jnp.bfloat16
F32 = jnp.float32
MB = 2**20
VM = pl.BlockSpec(memory_space=pltpu.VMEM)
SM = pl.BlockSpec(memory_space=pltpu.SMEM)
HB = pl.BlockSpec(memory_space=pltpu.HBM)
PEERS = 8
CORES = 2
HELD = 64
AUX = 4
CUT1, CUT2 = 3, 6


def iota(shape, dim):
    return lax.broadcasted_iota(jnp.int32, shape, dim)


def ones_where(mask):
    return jnp.where(mask, 1.0, 0.0).astype(BF)


def pack_kernel(d_in, out_ref, flat_ref, d_ref, sem):
    blocks, cells = d_ref.shape
    copy = pltpu.make_async_copy(d_in, d_ref, sem)
    copy.start()
    copy.wait()
    d = d_ref[...]
    for b in range(cells // 256):
        col = iota((1, 256), 1) + b * 256
        source = ((col & 31) << 5) + (col >> 5)
        y = jnp.zeros((blocks, 256), F32)
        for a in range(cells // 256):
            move = ones_where(iota((256, 256), 0) == source - a * 256)
            y += jnp.dot(d[:, a * 256:(a + 1) * 256], move, preferred_element_type=F32)
        for e in range(2):
            flat_ref[pl.ds(2 * b + e, blocks, stride=8), :] = y[:, e * 128:(e + 1) * 128]
    x = flat_ref[...].reshape(blocks, 8, 128).astype(BF)
    for p in range(out_ref.shape[0]):
        out_ref[p] = x


def run_pack(density, peers):
    blocks = density.shape[0]
    return pl.pallas_call(
        pack_kernel,
        out_shape=jax.ShapeDtypeStruct((peers, blocks, 8, 128), BF),
        in_specs=[HB],
        out_specs=VM,
        scratch_shapes=[pltpu.VMEM((blocks * 8, 128), F32), pltpu.VMEM(density.shape, BF), pltpu.SemaphoreType.DMA],
        compiler_params=pltpu.CompilerParams(vmem_limit_bytes=8 * MB),
    )(pltpu.with_memory_space_constraint(density, pltpu.HBM))


def lane_move():
    col = iota((1, 512), 1)
    source = ((col & 96) << 2) + ((col >> 7) << 5) + (col & 31)
    return ones_where(iota((512, 512), 0) == source)


def put_rows(y_ref, full, q, count):
    for e in range(2):
        v = 2 * q + e
        for mt in range(count):
            y_ref[mt * 64 + v * 8:mt * 64 + v * 8 + 8, :] = full[mt * 8:mt * 8 + 8, e * 128:(e + 1) * 128]


def gather_rows(y_ref, x_ref, first, count):
    for mt in range(first, first + count):
        for m in range(4):
            pair = [y_ref[pl.ds(mt * 64 + 4 * h + m, 8, stride=8), :] for h in range(2)]
            x_ref[mt * 16:(mt + 1) * 16, m * 128:(m + 1) * 128] = jnp.concatenate(pair, axis=0).astype(BF)


def turned(x_ref, move_ref, first, tiles):
    z = jnp.dot(x_ref[first * 16:(first + tiles) * 16, :], move_ref[...], preferred_element_type=F32)
    blocks = []
    for s in range(tiles):
        halves = []
        for h in range(2):
            row = (s * 2 + h) * 8
            halves.append(jnp.concatenate([z[row:row + 8, c * 128:(c + 1) * 128] for c in range(4)], axis=0))
        blocks.append(jnp.concatenate(halves, axis=1).astype(BF))
    return blocks


def lefts_kernel(me_ref, owner_in, slot_in, left_in, right_in, aux_in, dest_in, coeffs_ref,
                 l_out, table_ref, names_ref, owner_ref, slot_ref, left_ref, right_ref, aux_ref, dest_ref, i_sem, count_ref, y0_ref, y1_ref, x0_ref, x1_ref, move_ref, lw_ref, l_ref, l_sem):
    blocks, na, cells = coeffs_ref.shape
    tiles = na // 8
    tasks = slot_ref.shape[0]
    share = tasks // blocks
    peers, cap = PEERS, 128 // PEERS
    sub, lane = iota((8, 128), 0), iota((8, 128), 1)
    me = me_ref[0]
    indices = [
        pltpu.make_async_copy(x_in, x_ref, i_sem.at[n])
        for n, (x_in, x_ref) in enumerate(
            ((owner_in, owner_ref), (slot_in, slot_ref), (left_in, left_ref), (right_in, right_ref), (aux_in, aux_ref), (dest_in, dest_ref))
        )
    ]
    for copy in indices:
        copy.start()
    for b in range(peers):
        count_ref[b] = 0
    move_ref[...] = lane_move()
    for copy in indices:
        copy.wait()

    def place_some(r, names):
        for u in range(share):
            t = r * share + u
            dest = dest_ref[t]
            peer = lax.rem(dest, peers)
            place = count_ref[peer]
            count_ref[peer] = place + 1
            owner = owner_ref[t]
            table_ref[t] = lax.rem(owner + me, CORES) * (HELD * peers // CORES) + owner // CORES * HELD + slot_ref[t]
            table_ref[tasks + t] = right_ref[t] * AUX + aux_ref[t]
            table_ref[2 * tasks + t] = left_ref[t]
            table_ref[3 * tasks + t] = peer * (cap + 1) + place
            name = (dest // peers + 1).astype(F32)
            names = jnp.where((sub == peer) & (lane == me * cap + place), name, names)
        return names

    def two(h, names):
        for e, (y_ref, x_ref) in enumerate(((y0_ref, x0_ref), (y1_ref, x1_ref))):
            r = 2 * h + e
            for q in range(cells // 256):
                put_rows(y_ref, coeffs_ref[r, :, q * 256:(q + 1) * 256].astype(F32), q, tiles)
            gather_rows(y_ref, x_ref, 0, tiles)
            for s, block in enumerate(turned(x_ref, move_ref, 0, tiles)):
                lw_ref[s, pl.ds(pl.multiple_of(r * 32, 32), 32), :] = block
            names = place_some(r, names)
        return names

    names_ref[...] = lax.fori_loop(0, blocks // 2, two, jnp.zeros((8, 128), F32), unroll=4)
    copies = []
    for s in range(tiles):
        part = pl.ds(s * 256, 256)
        l_ref[part, :] = jnp.transpose(lw_ref[s])
        copies.append(pltpu.make_async_copy(l_ref.at[part], l_out.at[part], l_sem.at[s]))
        copies[s].start()
    for copy in copies:
        copy.wait()


def run_lefts(me, owner, slot, left, right, aux_of, dest, coeffs):
    blocks, na, cells = coeffs.shape
    tiles = na // 8
    indices = [pltpu.with_memory_space_constraint(x, pltpu.HBM) for x in (owner, slot, left, right, aux_of, dest)]
    return pl.pallas_call(
        lefts_kernel,
        out_shape=(
            pltpu.HBM((tiles * 256, blocks * 32), BF),
            jax.ShapeDtypeStruct((1024,), jnp.int32),
            jax.ShapeDtypeStruct((8, 128), F32),
        ),
        in_specs=[SM] + [HB] * 6 + [VM],
        out_specs=(HB, SM, VM),
        scratch_shapes=[pltpu.SMEM(x.shape, jnp.int32) for x in indices] + [
            pltpu.SemaphoreType.DMA((6,)),
            pltpu.SMEM((PEERS,), jnp.int32),
            pltpu.VMEM((na * 8, 128), F32),
            pltpu.VMEM((na * 8, 128), F32),
            pltpu.VMEM((na * 2, 512), BF),
            pltpu.VMEM((na * 2, 512), BF),
            pltpu.VMEM((512, 512), BF),
            pltpu.VMEM((tiles, blocks * 32, 256), BF),
            pltpu.VMEM((tiles * 256, blocks * 32), BF),
            pltpu.SemaphoreType.DMA((tiles,)),
        ],
        compiler_params=pltpu.CompilerParams(vmem_limit_bytes=16 * MB),
    )(me, *indices, coeffs)


def multiply(coeffs_ref, coulomb_ref, r, y_ref):
    cells = coeffs_ref.shape[2]
    count = coulomb_ref.shape[0] // 8
    for q in range(cells // 256):
        y = jnp.dot(coulomb_ref[...], coeffs_ref[r, :, q * 256:(q + 1) * 256], preferred_element_type=F32)
        put_rows(y_ref, y, q, count)


def turn(y_ref, x_ref, move_ref, w_ref, first, tiles):
    for a in range(y_ref.shape[0] // (64 * tiles)):
        gather_rows(y_ref, x_ref, a * tiles, tiles)
        for s, block in enumerate(turned(x_ref, move_ref, a * tiles, tiles)):
            w_ref[first + a, s * 32:(s + 1) * 32, :] = block


def rights_kernel(begin, end, coeffs_ref, coulomb_ref, after_ref, w_out, y0_ref, y1_ref, x0_ref, x1_ref, move_ref, w_ref, w_sem):
    na = coeffs_ref.shape[1]
    aux = coulomb_ref.shape[0] // na
    tiles = na // 8
    move_ref[...] = lane_move()
    ys, xs = (y0_ref, y1_ref), (x0_ref, x1_ref)
    copies = []
    multiply(coeffs_ref, coulomb_ref, begin, ys[0])
    for r in range(begin, end):
        e = (r - begin) % 2
        if r + 1 < end:
            multiply(coeffs_ref, coulomb_ref, r + 1, ys[1 - e])
        turn(ys[e], xs[e], move_ref, w_ref, (r - begin) * aux, tiles)
        part = pl.ds((r - begin) * aux, aux)
        copies.append(pltpu.make_async_copy(w_ref.at[part], w_out.at[part], w_sem.at[r - begin]))
        copies[-1].start()
    for copy in copies:
        copy.wait()


def rights_scratch(rows):
    return [
        pltpu.VMEM((rows * 8, 128), F32),
        pltpu.VMEM((rows * 8, 128), F32),
        pltpu.VMEM((rows * 2, 512), BF),
        pltpu.VMEM((rows * 2, 512), BF),
        pltpu.VMEM((512, 512), BF),
    ]


def run_rights(coeffs, vall, after, begin, end):
    na = coeffs.shape[1]
    aux = vall.shape[0] // na
    shape = ((end - begin) * aux, na // 8 * 32, 256)
    return pl.pallas_call(
        functools.partial(rights_kernel, begin, end),
        out_shape=pltpu.HBM(shape, BF),
        in_specs=[VM, VM, pl.BlockSpec(memory_space=pl.ANY)],
        out_specs=HB,
        scratch_shapes=rights_scratch(vall.shape[0]) + [
            pltpu.VMEM(shape, BF),
            pltpu.SemaphoreType.DMA((end - begin,)),
        ],
        compiler_params=pltpu.CompilerParams(vmem_limit_bytes=20 * MB),
    )(coeffs, vall, after)


def tasks_kernel(table_ref, names_ref, coeffs_ref, coulomb_ref, w1_in, w2_in, l_in, d_ref, e_ref,
                 out_ref, y0_ref, y1_ref, x0_ref, x1_ref, move_ref, dl_ref, a_ref, send_ref, w_ref, l_ref, sem):
    tiles = l_ref.shape[0] // 256
    blocks = l_ref.shape[1] // 32
    aux = w_ref.shape[0] // blocks
    tasks = dl_ref.shape[0] // 32
    groups = tasks // 8
    slots = out_ref.shape[1]
    half = d_ref.shape[0]

    here = pl.ds(0, w1_in.shape[0])
    there = pl.ds(w1_in.shape[0], w2_in.shape[0])
    copies = [
        pltpu.make_async_copy(l_in, l_ref, sem.at[0]),
        pltpu.make_async_copy(w1_in, w_ref.at[here], sem.at[1]),
        pltpu.make_async_copy(w2_in, w_ref.at[there], sem.at[2]),
    ]
    for i in (1, 2, 0):
        copies[i].start()
    move_ref[...] = lane_move()
    ys, xs = (y0_ref, y1_ref), (x0_ref, x1_ref)
    begin = (w1_in.shape[0] + w2_in.shape[0]) // aux
    for r in range(begin, blocks):
        multiply(coeffs_ref, coulomb_ref, r, ys[r % 2])
    for r in range(begin, blocks):
        turn(ys[r % 2], xs[r % 2], move_ref, w_ref, r * aux, tiles)
    send_ref[...] = jnp.zeros_like(send_ref)

    spread = ones_where((iota((256, 64), 0) >> 2) == iota((256, 64), 1))
    own_chunk = (iota((256, 128), 0) & 3) == (iota((256, 128), 1) >> 5)
    repeat = ones_where((iota((128, 256), 0) & 31) == (iota((128, 256), 1) & 31))
    for g in range(groups):
        picked = []
        for u in range(8):
            spot = table_ref[g * 8 + u]
            here = lax.rem(spot, half)
            picked.append(jnp.where(spot < half, d_ref[here].astype(F32), e_ref[here].astype(F32)))
        e = jnp.dot(spread, jnp.concatenate(picked, axis=0).astype(BF), preferred_element_type=F32)
        e = jnp.where(own_chunk, e, 0.0).astype(BF)
        dl_ref[g * 256:(g + 1) * 256, :] = jnp.dot(e, repeat, preferred_element_type=F32).astype(BF)

    diag = ones_where((iota((256, 256), 0) >> 5) == (iota((256, 256), 1) >> 5))
    fold = ones_where((iota((256, 128), 0) & 31) == (iota((256, 128), 1) & 31))
    chunk = iota((8, 128), 1) >> 5
    column = iota((32, 256), 1) >> 5

    def apply(g, carry):
        for u in range(64):
            t = g * 64 + u
            rows = pl.ds(pl.multiple_of(t * 32, 32), 32)
            bd = jnp.concatenate([dl_ref[rows, :]] * 8, axis=0) * diag
            y = jnp.dot(w_ref[table_ref[tasks + t]], bd, preferred_element_type=F32).astype(BF)
            for s in range(tiles):
                a_ref[rows, s * 256:(s + 1) * 256] = y[s * 32:(s + 1) * 32, :]
        return carry

    def close(g, carry):
        rows = pl.ds(pl.multiple_of(g * 2048, 2048), 2048)
        total = jnp.dot(a_ref[rows, :], l_ref[...], preferred_element_type=F32)
        own = [jnp.where(column == table_ref[2 * tasks + g * 64 + u], total[u * 32:(u + 1) * 32, :], 0.0) for u in range(64)]
        total = jnp.dot(jnp.concatenate(own, axis=0).astype(BF), fold, preferred_element_type=F32)
        for u in range(64):
            block = total[u * 32:u * 32 + 8, :]
            for q in range(1, 4):
                block = jnp.where(chunk == q, total[u * 32 + q * 8:u * 32 + q * 8 + 8, :], block)
            send_ref[table_ref[3 * tasks + g * 64 + u]] = block
        return carry

    copies[1].wait()
    copies[2].wait()
    lax.fori_loop(0, tasks // 64, apply, 0)
    copies[0].wait()
    lax.fori_loop(0, tasks // 64, close, 0)
    names = names_ref[...]
    for p in range(out_ref.shape[0]):
        send_ref[p * slots + slots - 1] = jnp.broadcast_to(names[p:p + 1, :], (8, 128))
    out_ref[...] = send_ref[...].reshape(out_ref.shape).astype(out_ref.dtype)


def run_tasks(table, names, coeffs, vall, w1, w2, l, dens, other, tasks, peers, cap):
    w1, w2, l = (pltpu.with_memory_space_constraint(x, pltpu.HBM) for x in (w1, w2, l))
    blocks, na, _ = coeffs.shape
    return pl.pallas_call(
        tasks_kernel,
        out_shape=jax.ShapeDtypeStruct((peers, cap + 1, 8, 128), BF),
        in_specs=[SM, VM, VM, VM, HB, HB, HB, VM, VM],
        out_specs=VM,
        scratch_shapes=rights_scratch(vall.shape[0]) + [
            pltpu.VMEM((tasks * 32, 256), BF),
            pltpu.VMEM((tasks * 32, l.shape[0]), BF),
            pltpu.VMEM((peers * (cap + 1), 8, 128), F32),
            pltpu.VMEM((blocks * (vall.shape[0] // na),) + w1.shape[1:], BF),
            pltpu.VMEM(l.shape, BF),
            pltpu.SemaphoreType.DMA((3,)),
        ],
        compiler_params=pltpu.CompilerParams(vmem_limit_bytes=40 * MB),
    )(table, names, coeffs, vall, w1, w2, l, dens, other)


def spread_kernel(recv_ref, out_ref, flat_ref):
    peers, slots = recv_ref.shape[0], recv_ref.shape[1]
    cap = slots - 1
    rows = out_ref.shape[0]
    names = recv_ref[0, cap].astype(F32)
    for p in range(1, peers):
        names = names + recv_ref[p, cap].astype(F32)
    names = jnp.broadcast_to(names[0:1, :], (rows, 128)).astype(jnp.int32)
    hot = ones_where(iota((rows, 128), 0) + 1 == names)
    for p in range(peers):
        for n in range(cap):
            flat_ref[(p * cap + n) * 8:(p * cap + n + 1) * 8, :] = recv_ref[p, n].astype(F32)
    sums = []
    for i in range(8):
        x = flat_ref[pl.ds(i, 128, stride=8), :]
        sums.append(jnp.dot(hot, x.astype(BF), preferred_element_type=F32))
    for i in range(8):
        flat_ref[pl.ds(i, rows, stride=8), :] = sums[i]
    out_ref[...] = flat_ref[0:rows * 8, :].reshape(rows, 8, 128).astype(out_ref.dtype)


def run_spread(recv, rows, dtype):
    peers, slots = recv.shape[:2]
    return pl.pallas_call(
        spread_kernel,
        out_shape=jax.ShapeDtypeStruct((rows, 8, 128), dtype),
        in_specs=[VM],
        out_specs=VM,
        scratch_shapes=[pltpu.VMEM((max(rows, peers * (slots - 1)) * 8, 128), F32)],
        compiler_params=pltpu.CompilerParams(vmem_limit_bytes=8 * MB),
    )(recv)


def exact_dot(x, y):
    out = None
    for _ in range(3):
        part = x.astype(BF)
        x = x - part.astype(F32)
        term = jnp.dot(part, y, preferred_element_type=F32)
        out = term if out is None else out + term
    return out


def final_kernel(recv_ref, out_ref):
    total = jnp.sum(recv_ref[...].astype(F32), axis=0) * -0.25
    vi = iota((64, 128), 0) >> 3
    wide = jnp.concatenate([total] * 8, axis=0)
    wide = jnp.where((iota((64, 128), 1) & 7) == vi, wide, 0.0)
    r, c = iota((128, 128), 0), iota((128, 128), 1)
    move = ones_where((r >> 3) == ((c & 3) << 2) + (c >> 5))
    wide = exact_dot(wide, move)
    wide = jnp.where(((iota((64, 128), 1) >> 2) & 7) == (iota((64, 128), 0) & 7), wide, 0.0)
    out_ref[...] = jnp.sum(wide.reshape(8, 8, 128), axis=1)


def run_final(recv):
    return pl.pallas_call(
        final_kernel,
        out_shape=jax.ShapeDtypeStruct((8, 128), F32),
        in_specs=[VM],
        out_specs=VM,
        compiler_params=pltpu.CompilerParams(vmem_limit_bytes=4 * MB),
    )(recv)


def per_device(coeffs, coulomb, density, task_owner, task_slot, task_left, task_right, task_aux, task_dest):
    na = coeffs.shape[1]
    blk, task = lax.axis_size("x") * lax.axis_size("core"), lax.axis_size("task")
    chips = blk // CORES
    dens = lax.all_to_all(run_pack(density, chips), "x", 0, 0, tiled=True)
    me = lax.axis_index(BLK).astype(jnp.int32).reshape(1)
    vall = coulomb.reshape(coulomb.shape[0] * na, na)
    l, table, names = run_lefts(me, task_owner.reshape(-1), task_slot, task_left, task_right, task_aux, task_dest, coeffs)
    w1 = run_rights(coeffs, vall, names, 0, CUT1)
    dens = dens.reshape(chips * HELD, 8, 128)
    dens, l, table, names, w1 = lax.optimization_barrier((dens, l, table, names, w1))
    other = lax.ppermute(dens, "core", [(0, 1), (1, 0)])
    w2 = run_rights(coeffs, vall, dens, CUT1, CUT2)
    send = run_tasks(table, names, coeffs, vall, w1, w2, l, dens, other, task_slot.shape[0], blk, 128 // blk)
    recv = lax.all_to_all(send, BLK, 0, 0, tiled=True)
    rows = run_spread(recv, task, BF)
    back = lax.all_to_all(rows, "task", 0, 0, tiled=True)
    return run_final(back).reshape(1, density.shape[1])


BLK = ("x", "core")


def solution(mesh):
    sizes = (mesh.shape["task"], mesh.shape["blk"] // CORES, CORES)
    fine = jax.sharding.Mesh(mesh.devices.reshape(sizes), ("task", "x", "core"))
    every = P(("task", "x", "core"))
    placed = (every, every, P(BLK), every, every, every, every, every, every)
    return jax.shard_map(per_device, mesh=fine, in_specs=placed, out_specs=every, check_vma=False)
```

```python
import functools
import math

import jax
import jax.numpy as jnp
from jax import lax
from jax.experimental import pallas as pl
from jax.experimental.pallas import tpu as pltpu
from jax.sharding import PartitionSpec as P

BF = jnp.bfloat16
F32 = jnp.float32
MB = 2**20
VM = pl.BlockSpec(memory_space=pltpu.VMEM)
SM = pl.BlockSpec(memory_space=pltpu.SMEM)
HB = pl.BlockSpec(memory_space=pltpu.HBM)
PEERS = 8
CORES = 2
HELD = 64
AUX = 4
CUT1, CUT2 = 3, 7


def iota(shape, dim):
    return lax.broadcasted_iota(jnp.int32, shape, dim)


def ones_where(mask):
    return jnp.where(mask, 1.0, 0.0).astype(BF)


def pack_kernel(d_in, out_ref, flat_ref, d_ref, move_ref, sem):
    blocks, cells = d_ref.shape
    copy = pltpu.make_async_copy(d_in, d_ref, sem)
    copy.start()
    for a in range(cells // 256):
        for b in range(cells // 256):
            col = iota((1, 256), 1) + b * 256
            source = ((col & 31) << 5) + (col >> 5) - a * 256
            move_ref[a * 4 + b] = ones_where(iota((256, 256), 0) == source)
    copy.wait()
    d = d_ref[...]
    for b in range(cells // 256):
        y = jnp.zeros((blocks, 256), F32)
        for a in range(cells // 256):
            y += jnp.dot(d[:, a * 256:(a + 1) * 256], move_ref[a * 4 + b], preferred_element_type=F32)
        for e in range(2):
            flat_ref[pl.ds(2 * b + e, blocks, stride=8), :] = y[:, e * 128:(e + 1) * 128]
    x = flat_ref[...].reshape(blocks, 8, 128).astype(BF)
    for p in range(out_ref.shape[0]):
        out_ref[p] = x


def run_pack(density, peers):
    blocks = density.shape[0]
    return pl.pallas_call(
        pack_kernel,
        out_shape=jax.ShapeDtypeStruct((peers, blocks, 8, 128), BF),
        in_specs=[HB],
        out_specs=VM,
        scratch_shapes=[pltpu.VMEM((blocks * 8, 128), F32), pltpu.VMEM(density.shape, BF),
                        pltpu.VMEM((16, 256, 256), BF), pltpu.SemaphoreType.DMA],
        compiler_params=pltpu.CompilerParams(vmem_limit_bytes=8 * MB),
    )(pltpu.with_memory_space_constraint(density, pltpu.HBM))


def lane_move():
    col = iota((1, 512), 1)
    source = ((col & 96) << 2) + ((col >> 7) << 5) + (col & 31)
    return ones_where(iota((512, 512), 0) == source)


def put_rows(y_ref, full, q, count):
    for e in range(2):
        v = 2 * q + e
        for mt in range(count):
            y_ref[mt * 64 + v * 8:mt * 64 + v * 8 + 8, :] = full[mt * 8:mt * 8 + 8, e * 128:(e + 1) * 128]


def gather_rows(y_ref, x_ref, first, count):
    for mt in range(first, first + count):
        for m in range(4):
            pair = [y_ref[pl.ds(mt * 64 + 4 * h + m, 8, stride=8), :] for h in range(2)]
            x_ref[mt * 16:(mt + 1) * 16, m * 128:(m + 1) * 128] = jnp.concatenate(pair, axis=0).astype(BF)


def turned(x_ref, move_ref, first, tiles):
    z = jnp.dot(x_ref[first * 16:(first + tiles) * 16, :], move_ref[...], preferred_element_type=F32)
    blocks = []
    for s in range(tiles):
        halves = []
        for h in range(2):
            row = (s * 2 + h) * 8
            halves.append(jnp.concatenate([z[row:row + 8, c * 128:(c + 1) * 128] for c in range(4)], axis=0))
        blocks.append(jnp.concatenate(halves, axis=1).astype(BF))
    return blocks


def lefts_kernel(deep, wide, me_ref, owner_in, slot_in, left_in, right_in, aux_in, dest_in, coeffs_ref,
                 l_out, table_ref, names_ref, owner_ref, slot_ref, left_ref, right_ref, aux_ref, dest_ref, i_sem, count_ref, y0_ref, y1_ref, x0_ref, x1_ref, move_ref, lw_ref, l_ref, l_sem):
    blocks, na, cells = coeffs_ref.shape
    tiles = na // 8
    tasks = slot_ref.shape[0]
    share = tasks // blocks
    peers, cap = PEERS, 128 // PEERS
    sub, lane = iota((8, 128), 0), iota((8, 128), 1)
    me = me_ref[0]
    indices = [
        pltpu.make_async_copy(x_in, x_ref, i_sem.at[n])
        for n, (x_in, x_ref) in enumerate(
            ((owner_in, owner_ref), (slot_in, slot_ref), (left_in, left_ref), (right_in, right_ref), (aux_in, aux_ref), (dest_in, dest_ref))
        )
    ]
    for copy in indices:
        copy.start()
    for b in range(peers):
        count_ref[b] = 0
    move_ref[...] = lane_move()
    for copy in indices:
        copy.wait()

    def place_some(r, names):
        for u in range(share):
            t = r * share + u
            dest = dest_ref[t]
            peer = lax.rem(dest, peers)
            place = count_ref[peer]
            count_ref[peer] = place + 1
            owner = owner_ref[t]
            table_ref[t] = lax.rem(owner + me, CORES) * (HELD * peers // CORES) + owner // CORES * HELD + slot_ref[t]
            table_ref[tasks + t] = right_ref[t] * AUX + aux_ref[t]
            table_ref[2 * tasks + t] = left_ref[t]
            table_ref[3 * tasks + t] = peer * (cap + 1) + place
            task = lax.div(dest, peers)
            name = (lax.rem(task, wide) * deep + lax.div(task, wide) + 1).astype(F32)
            names = jnp.where((sub == peer) & (lane == me * cap + place), name, names)
        return names

    def two(h, names):
        for e, (y_ref, x_ref) in enumerate(((y0_ref, x0_ref), (y1_ref, x1_ref))):
            r = 2 * h + e
            for q in range(cells // 256):
                put_rows(y_ref, coeffs_ref[r, :, q * 256:(q + 1) * 256].astype(F32), q, tiles)
            gather_rows(y_ref, x_ref, 0, tiles)
            for s, block in enumerate(turned(x_ref, move_ref, 0, tiles)):
                lw_ref[s, pl.ds(pl.multiple_of(r * 32, 32), 32), :] = block
            names = place_some(r, names)
        return names

    names_ref[...] = lax.fori_loop(0, blocks // 2, two, jnp.zeros((8, 128), F32), unroll=4)
    copies = []
    for s in range(tiles):
        part = pl.ds(s * 256, 256)
        l_ref[part, :] = jnp.transpose(lw_ref[s])
        copies.append(pltpu.make_async_copy(l_ref.at[part], l_out.at[part], l_sem.at[s]))
        copies[s].start()
    for copy in copies:
        copy.wait()


def run_lefts(deep, wide, me, owner, slot, left, right, aux_of, dest, coeffs):
    blocks, na, cells = coeffs.shape
    tiles = na // 8
    indices = [pltpu.with_memory_space_constraint(x, pltpu.HBM) for x in (owner, slot, left, right, aux_of, dest)]
    return pl.pallas_call(
        functools.partial(lefts_kernel, deep, wide),
        out_shape=(
            pltpu.HBM((tiles * 256, blocks * 32), BF),
            jax.ShapeDtypeStruct((1024,), jnp.int32),
            jax.ShapeDtypeStruct((8, 128), F32),
        ),
        in_specs=[SM] + [HB] * 6 + [VM],
        out_specs=(HB, SM, VM),
        scratch_shapes=[pltpu.SMEM(x.shape, jnp.int32) for x in indices] + [
            pltpu.SemaphoreType.DMA((6,)),
            pltpu.SMEM((PEERS,), jnp.int32),
            pltpu.VMEM((na * 8, 128), F32),
            pltpu.VMEM((na * 8, 128), F32),
            pltpu.VMEM((na * 2, 512), BF),
            pltpu.VMEM((na * 2, 512), BF),
            pltpu.VMEM((512, 512), BF),
            pltpu.VMEM((tiles, blocks * 32, 256), BF),
            pltpu.VMEM((tiles * 256, blocks * 32), BF),
            pltpu.SemaphoreType.DMA((tiles,)),
        ],
        compiler_params=pltpu.CompilerParams(vmem_limit_bytes=16 * MB),
    )(me, *indices, coeffs)


def multiply(coeffs_ref, coulomb_ref, r, y_ref):
    cells = coeffs_ref.shape[2]
    count = coulomb_ref.shape[0] // 8
    for q in range(cells // 256):
        y = jnp.dot(coulomb_ref[...], coeffs_ref[r, :, q * 256:(q + 1) * 256], preferred_element_type=F32)
        put_rows(y_ref, y, q, count)


def turn(y_ref, x_ref, move_ref, w_ref, first, tiles):
    for a in range(y_ref.shape[0] // (64 * tiles)):
        gather_rows(y_ref, x_ref, a * tiles, tiles)
        for s, block in enumerate(turned(x_ref, move_ref, a * tiles, tiles)):
            w_ref[first + a, s * 32:(s + 1) * 32, :] = block


def rights_kernel(begin, end, coeffs_ref, coulomb_ref, after_ref, w_out, y0_ref, y1_ref, x0_ref, x1_ref, move_ref, w_ref, w_sem):
    na = coeffs_ref.shape[1]
    aux = coulomb_ref.shape[0] // na
    tiles = na // 8
    move_ref[...] = lane_move()
    ys, xs = (y0_ref, y1_ref), (x0_ref, x1_ref)
    copies = []
    multiply(coeffs_ref, coulomb_ref, begin, ys[0])
    for r in range(begin, end):
        e = (r - begin) % 2
        if r + 1 < end:
            multiply(coeffs_ref, coulomb_ref, r + 1, ys[1 - e])
        turn(ys[e], xs[e], move_ref, w_ref, (r - begin) * aux, tiles)
        part = pl.ds((r - begin) * aux, aux)
        copies.append(pltpu.make_async_copy(w_ref.at[part], w_out.at[part], w_sem.at[r - begin]))
        copies[-1].start()
    for copy in copies:
        copy.wait()


def rights_scratch(rows):
    return [
        pltpu.VMEM((rows * 8, 128), F32),
        pltpu.VMEM((rows * 8, 128), F32),
        pltpu.VMEM((rows * 2, 512), BF),
        pltpu.VMEM((rows * 2, 512), BF),
        pltpu.VMEM((512, 512), BF),
    ]


def run_rights(coeffs, vall, after, begin, end):
    na = coeffs.shape[1]
    aux = vall.shape[0] // na
    shape = ((end - begin) * aux, na // 8 * 32, 256)
    return pl.pallas_call(
        functools.partial(rights_kernel, begin, end),
        out_shape=pltpu.HBM(shape, BF),
        in_specs=[VM, VM, pl.BlockSpec(memory_space=pl.ANY)],
        out_specs=HB,
        scratch_shapes=rights_scratch(vall.shape[0]) + [
            pltpu.VMEM(shape, BF),
            pltpu.SemaphoreType.DMA((end - begin,)),
        ],
        compiler_params=pltpu.CompilerParams(vmem_limit_bytes=20 * MB),
    )(coeffs, vall, after)


def near_kernel(begin, end, coeffs_ref, coulomb_ref, after_ref, w_ref, y0_ref, y1_ref, x0_ref, x1_ref, move_ref):
    na = coeffs_ref.shape[1]
    aux = coulomb_ref.shape[0] // na
    move_ref[...] = lane_move()
    ys, xs = (y0_ref, y1_ref), (x0_ref, x1_ref)
    multiply(coeffs_ref, coulomb_ref, begin, ys[0])
    for r in range(begin, end):
        e = (r - begin) % 2
        if r + 1 < end:
            multiply(coeffs_ref, coulomb_ref, r + 1, ys[1 - e])
        turn(ys[e], xs[e], move_ref, w_ref, (r - begin) * aux, na // 8)


def run_near(coeffs, vall, after, begin, end):
    na = coeffs.shape[1]
    aux = vall.shape[0] // na
    return pl.pallas_call(
        functools.partial(near_kernel, begin, end),
        out_shape=jax.ShapeDtypeStruct(((end - begin) * aux, na // 8 * 32, 256), BF),
        in_specs=[VM, VM, pl.BlockSpec(memory_space=pl.ANY)],
        out_specs=VM,
        scratch_shapes=rights_scratch(vall.shape[0]),
        compiler_params=pltpu.CompilerParams(vmem_limit_bytes=20 * MB),
    )(coeffs, vall, after)


def tasks_kernel(table_ref, names_ref, coeffs_ref, coulomb_ref, w1_in, w2_in, l_in, d_ref, e_ref,
                 out_ref, y0_ref, y1_ref, x0_ref, x1_ref, move_ref, dl_ref, a_ref, send_ref, w_ref, l_ref, sem):
    tiles = l_ref.shape[0] // 256
    blocks = l_ref.shape[1] // 32
    aux = w_ref.shape[0] // blocks
    tasks = dl_ref.shape[0] // 32
    groups = tasks // 8
    slots = out_ref.shape[1]
    half = d_ref.shape[0]

    here = pl.ds(0, w1_in.shape[0])
    there = pl.ds(w1_in.shape[0], w2_in.shape[0])
    copies = [
        pltpu.make_async_copy(l_in, l_ref, sem.at[0]),
        pltpu.make_async_copy(w1_in, w_ref.at[here], sem.at[1]),
        pltpu.make_async_copy(w2_in, w_ref.at[there], sem.at[2]),
    ]
    for i in (1, 0, 2):
        copies[i].start()
    move_ref[...] = lane_move()
    ys, xs = (y0_ref, y1_ref), (x0_ref, x1_ref)
    begin = (w1_in.shape[0] + w2_in.shape[0]) // aux
    for r in range(begin, blocks):
        multiply(coeffs_ref, coulomb_ref, r, ys[r % 2])
    for r in range(begin, blocks):
        turn(ys[r % 2], xs[r % 2], move_ref, w_ref, r * aux, tiles)
    send_ref[...] = jnp.zeros_like(send_ref)

    spread = ones_where((iota((256, 64), 0) >> 2) == iota((256, 64), 1))
    own_chunk = (iota((256, 128), 0) & 3) == (iota((256, 128), 1) >> 5)
    repeat = ones_where((iota((128, 256), 0) & 31) == (iota((128, 256), 1) & 31))
    for g in range(groups):
        picked = []
        for u in range(8):
            spot = table_ref[g * 8 + u]
            here = lax.rem(spot, half)
            picked.append(jnp.where(spot < half, d_ref[here].astype(F32), e_ref[here].astype(F32)))
        e = jnp.dot(spread, jnp.concatenate(picked, axis=0).astype(BF), preferred_element_type=F32)
        e = jnp.where(own_chunk, e, 0.0).astype(BF)
        dl_ref[g * 256:(g + 1) * 256, :] = jnp.dot(e, repeat, preferred_element_type=F32).astype(BF)

    diag = ones_where((iota((256, 256), 0) >> 5) == (iota((256, 256), 1) >> 5))
    fold = ones_where((iota((256, 128), 0) & 31) == (iota((256, 128), 1) & 31))
    chunk = iota((8, 128), 1) >> 5
    column = iota((32, 256), 1) >> 5

    def apply(g, carry):
        for u in range(64):
            t = g * 64 + u
            rows = pl.ds(pl.multiple_of(t * 32, 32), 32)
            bd = jnp.concatenate([dl_ref[rows, :]] * 8, axis=0) * diag
            y = jnp.dot(w_ref[table_ref[tasks + t]], bd, preferred_element_type=F32).astype(BF)
            for s in range(tiles):
                a_ref[rows, s * 256:(s + 1) * 256] = y[s * 32:(s + 1) * 32, :]
        return carry

    def close(g, carry):
        rows = pl.ds(pl.multiple_of(g * 2048, 2048), 2048)
        total = jnp.dot(a_ref[rows, :], l_ref[...], preferred_element_type=F32)
        own = [jnp.where(column == table_ref[2 * tasks + g * 64 + u], total[u * 32:(u + 1) * 32, :], 0.0) for u in range(64)]
        total = jnp.dot(jnp.concatenate(own, axis=0).astype(BF), fold, preferred_element_type=F32)
        for u in range(64):
            block = total[u * 32:u * 32 + 8, :]
            for q in range(1, 4):
                block = jnp.where(chunk == q, total[u * 32 + q * 8:u * 32 + q * 8 + 8, :], block)
            send_ref[table_ref[3 * tasks + g * 64 + u]] = block
        return carry

    copies[1].wait()
    copies[2].wait()
    lax.fori_loop(0, tasks // 64, apply, 0)
    copies[0].wait()
    lax.fori_loop(0, tasks // 64, close, 0)
    names = names_ref[...]
    for p in range(out_ref.shape[0]):
        send_ref[p * slots + slots - 1] = jnp.broadcast_to(names[p:p + 1, :], (8, 128))
    out_ref[...] = send_ref[...].reshape(out_ref.shape).astype(out_ref.dtype)


def run_tasks(table, names, coeffs, vall, w1, w2, l, dens, other, tasks, peers, cap):
    w1, l = (pltpu.with_memory_space_constraint(x, pltpu.HBM) for x in (w1, l))
    blocks, na, _ = coeffs.shape
    return pl.pallas_call(
        tasks_kernel,
        out_shape=jax.ShapeDtypeStruct((peers, cap + 1, 8, 128), BF),
        in_specs=[SM, VM, VM, VM, HB, pl.BlockSpec(memory_space=pl.ANY), HB, VM, VM],
        out_specs=VM,
        scratch_shapes=rights_scratch(vall.shape[0]) + [
            pltpu.VMEM((tasks * 32, 256), BF),
            pltpu.VMEM((tasks * 32, l.shape[0]), BF),
            pltpu.VMEM((peers * (cap + 1), 8, 128), F32),
            pltpu.VMEM((blocks * (vall.shape[0] // na),) + w1.shape[1:], BF),
            pltpu.VMEM(l.shape, BF),
            pltpu.SemaphoreType.DMA((3,)),
        ],
        compiler_params=pltpu.CompilerParams(vmem_limit_bytes=40 * MB),
    )(table, names, coeffs, vall, w1, w2, l, dens, other)


def spread_kernel(recv_ref, out_ref, flat_ref):
    peers, slots = recv_ref.shape[0], recv_ref.shape[1]
    cap = slots - 1
    rows = out_ref.shape[0]
    names = recv_ref[0, cap].astype(F32)
    for p in range(1, peers):
        names = names + recv_ref[p, cap].astype(F32)
    names = jnp.broadcast_to(names[0:1, :], (rows, 128)).astype(jnp.int32)
    hot = ones_where(iota((rows, 128), 0) + 1 == names)
    for p in range(peers):
        for n in range(cap):
            flat_ref[(p * cap + n) * 8:(p * cap + n + 1) * 8, :] = recv_ref[p, n].astype(F32)
    sums = []
    for i in range(8):
        x = flat_ref[pl.ds(i, 128, stride=8), :]
        sums.append(jnp.dot(hot, x.astype(BF), preferred_element_type=F32))
    for i in range(8):
        flat_ref[pl.ds(i, rows, stride=8), :] = sums[i]
    out_ref[...] = flat_ref[0:rows * 8, :].reshape(rows, 8, 128).astype(out_ref.dtype)


def run_spread(recv, rows, dtype):
    peers, slots = recv.shape[:2]
    return pl.pallas_call(
        spread_kernel,
        out_shape=jax.ShapeDtypeStruct((rows, 8, 128), dtype),
        in_specs=[VM],
        out_specs=VM,
        scratch_shapes=[pltpu.VMEM((max(rows, peers * (slots - 1)) * 8, 128), F32)],
        compiler_params=pltpu.CompilerParams(vmem_limit_bytes=8 * MB),
    )(recv)


def exact_dot(x, y):
    out = None
    for _ in range(3):
        part = x.astype(BF)
        x = x - part.astype(F32)
        term = jnp.dot(part, y, preferred_element_type=F32)
        out = term if out is None else out + term
    return out


def final_kernel(recv_ref, out_ref):
    total = jnp.sum(recv_ref[...].astype(F32), axis=0) * -0.25
    vi = iota((64, 128), 0) >> 3
    wide = jnp.concatenate([total] * 8, axis=0)
    wide = jnp.where((iota((64, 128), 1) & 7) == vi, wide, 0.0)
    r, c = iota((128, 128), 0), iota((128, 128), 1)
    move = ones_where((r >> 3) == ((c & 3) << 2) + (c >> 5))
    wide = exact_dot(wide, move)
    wide = jnp.where(((iota((64, 128), 1) >> 2) & 7) == (iota((64, 128), 0) & 7), wide, 0.0)
    out_ref[...] = jnp.sum(wide.reshape(8, 8, 128), axis=1)


def run_final(recv):
    return pl.pallas_call(
        final_kernel,
        out_shape=jax.ShapeDtypeStruct((8, 128), F32),
        in_specs=[VM],
        out_specs=VM,
        compiler_params=pltpu.CompilerParams(vmem_limit_bytes=4 * MB),
    )(recv)


def per_device(coeffs, coulomb, density, task_owner, task_slot, task_left, task_right, task_aux, task_dest):
    na = coeffs.shape[1]
    blk, task = lax.axis_size("x") * lax.axis_size("core"), lax.axis_size("z") * lax.axis_size("y")
    chips = blk // CORES
    dens = lax.all_to_all(run_pack(density, chips), "x", 0, 0, tiled=True)
    me = lax.axis_index(BLK).astype(jnp.int32).reshape(1)
    vall = coulomb.reshape(coulomb.shape[0] * na, na)
    l, table, names = run_lefts(lax.axis_size("z"), lax.axis_size("y"), me, task_owner.reshape(-1), task_slot, task_left, task_right, task_aux, task_dest, coeffs)
    w1 = run_rights(coeffs, vall, names, 0, CUT1)
    dens = dens.reshape(chips * HELD, 8, 128)
    dens, l, table, names, w1 = lax.optimization_barrier((dens, l, table, names, w1))
    other = lax.ppermute(dens, "core", [(0, 1), (1, 0)])
    w2 = run_near(coeffs, vall, dens, CUT1, CUT2)
    send = run_tasks(table, names, coeffs, vall, w1, w2, l, dens, other, task_slot.shape[0], blk, 128 // blk)
    recv = lax.all_to_all(send, BLK, 0, 0, tiled=True)
    rows = run_spread(recv, task, BF)
    back = lax.all_to_all(rows, ("y", "z"), 0, 0, tiled=True)
    return run_final(back).reshape(1, density.shape[1])


BLK = ("x", "core")


def solution(mesh):
    wide = math.gcd(mesh.shape["task"], 8)
    sizes = (mesh.shape["task"] // wide, wide, mesh.shape["blk"] // CORES, CORES)
    fine = jax.sharding.Mesh(mesh.devices.reshape(sizes), ("z", "y", "x", "core"))
    every = P(("z", "y", "x", "core"))
    placed = (every, every, P(BLK), every, every, every, every, every, every)
    return jax.shard_map(per_device, mesh=fine, in_specs=placed, out_specs=every, check_vma=False)
```

```python
import functools
import math

import jax
import jax.numpy as jnp
from jax import lax
from jax.experimental import pallas as pl
from jax.experimental.pallas import tpu as pltpu
from jax.sharding import PartitionSpec as P

BF = jnp.bfloat16
F32 = jnp.float32
MB = 2**20
VM = pl.BlockSpec(memory_space=pltpu.VMEM)
SM = pl.BlockSpec(memory_space=pltpu.SMEM)
HB = pl.BlockSpec(memory_space=pltpu.HBM)
PEERS = 8
CORES = 2
HELD = 64
AUX = 4
CUT1, CUT2 = 3, 7


def iota(shape, dim):
    return lax.broadcasted_iota(jnp.int32, shape, dim)


def ones_where(mask):
    return jnp.where(mask, 1.0, 0.0).astype(BF)


def pack_kernel(d_in, out_ref, flat_ref, d_ref, move_ref, sem):
    blocks, cells = d_ref.shape
    copy = pltpu.make_async_copy(d_in, d_ref, sem)
    copy.start()
    for a in range(cells // 256):
        for b in range(cells // 256):
            col = iota((1, 256), 1) + b * 256
            source = ((col & 31) << 5) + (col >> 5) - a * 256
            move_ref[a * 4 + b] = ones_where(iota((256, 256), 0) == source)
    copy.wait()
    d = d_ref[...]
    for b in range(cells // 256):
        y = jnp.zeros((blocks, 256), F32)
        for a in range(cells // 256):
            y += jnp.dot(d[:, a * 256:(a + 1) * 256], move_ref[a * 4 + b], preferred_element_type=F32)
        for e in range(2):
            flat_ref[pl.ds(2 * b + e, blocks, stride=8), :] = y[:, e * 128:(e + 1) * 128]
    x = flat_ref[...].reshape(blocks, 8, 128).astype(BF)
    for p in range(out_ref.shape[0]):
        out_ref[p] = x


def run_pack(density, peers):
    blocks = density.shape[0]
    return pl.pallas_call(
        pack_kernel,
        out_shape=jax.ShapeDtypeStruct((peers, blocks, 8, 128), BF),
        in_specs=[HB],
        out_specs=VM,
        scratch_shapes=[pltpu.VMEM((blocks * 8, 128), F32), pltpu.VMEM(density.shape, BF),
                        pltpu.VMEM((16, 256, 256), BF), pltpu.SemaphoreType.DMA],
        compiler_params=pltpu.CompilerParams(vmem_limit_bytes=8 * MB),
    )(pltpu.with_memory_space_constraint(density, pltpu.HBM))


def lane_move():
    col = iota((1, 512), 1)
    source = ((col & 96) << 2) + ((col >> 7) << 5) + (col & 31)
    return ones_where(iota((512, 512), 0) == source)


def put_rows(y_ref, full, q, count):
    for e in range(2):
        v = 2 * q + e
        for mt in range(count):
            y_ref[mt * 64 + v * 8:mt * 64 + v * 8 + 8, :] = full[mt * 8:mt * 8 + 8, e * 128:(e + 1) * 128]


def gather_rows(y_ref, x_ref, first, count):
    for mt in range(first, first + count):
        for m in range(4):
            pair = [y_ref[pl.ds(mt * 64 + 4 * h + m, 8, stride=8), :] for h in range(2)]
            x_ref[mt * 16:(mt + 1) * 16, m * 128:(m + 1) * 128] = jnp.concatenate(pair, axis=0).astype(BF)


def turned(x_ref, move_ref, first, tiles):
    z = jnp.dot(x_ref[first * 16:(first + tiles) * 16, :], move_ref[...], preferred_element_type=F32)
    blocks = []
    for s in range(tiles):
        halves = []
        for h in range(2):
            row = (s * 2 + h) * 8
            halves.append(jnp.concatenate([z[row:row + 8, c * 128:(c + 1) * 128] for c in range(4)], axis=0))
        blocks.append(jnp.concatenate(halves, axis=1).astype(BF))
    return blocks


def lefts_kernel(deep, wide, me_ref, owner_in, slot_in, left_in, right_in, aux_in, dest_in, coeffs_ref,
                 l_out, table_ref, names_ref, owner_ref, slot_ref, left_ref, right_ref, aux_ref, dest_ref, i_sem, count_ref, y0_ref, y1_ref, x0_ref, x1_ref, move_ref, lw_ref, l_ref, l_sem):
    blocks, na, cells = coeffs_ref.shape
    tiles = na // 8
    tasks = slot_ref.shape[0]
    share = tasks // blocks
    peers, cap = PEERS, 128 // PEERS
    sub, lane = iota((8, 128), 0), iota((8, 128), 1)
    me = me_ref[0]
    indices = [
        pltpu.make_async_copy(x_in, x_ref, i_sem.at[n])
        for n, (x_in, x_ref) in enumerate(
            ((owner_in, owner_ref), (slot_in, slot_ref), (left_in, left_ref), (right_in, right_ref), (aux_in, aux_ref), (dest_in, dest_ref))
        )
    ]
    for copy in indices:
        copy.start()
    for b in range(peers):
        count_ref[b] = 0
    move_ref[...] = lane_move()
    for copy in indices:
        copy.wait()

    def place_some(r, names):
        for u in range(share):
            t = r * share + u
            dest = dest_ref[t]
            peer = lax.rem(dest, peers)
            place = count_ref[peer]
            count_ref[peer] = place + 1
            owner = owner_ref[t]
            table_ref[t] = lax.rem(owner + me, CORES) * (HELD * peers // CORES) + owner // CORES * HELD + slot_ref[t]
            table_ref[tasks + t] = right_ref[t] * AUX + aux_ref[t]
            table_ref[2 * tasks + t] = left_ref[t]
            table_ref[3 * tasks + t] = peer * (cap + 1) + place
            task = lax.div(dest, peers)
            name = (lax.rem(task, wide) * deep + lax.div(task, wide) + 1).astype(F32)
            names = jnp.where((sub == peer) & (lane == me * cap + place), name, names)
        return names

    def two(h, names):
        for e, (y_ref, x_ref) in enumerate(((y0_ref, x0_ref), (y1_ref, x1_ref))):
            r = 2 * h + e
            for q in range(cells // 256):
                put_rows(y_ref, coeffs_ref[r, :, q * 256:(q + 1) * 256].astype(F32), q, tiles)
            gather_rows(y_ref, x_ref, 0, tiles)
            for s, block in enumerate(turned(x_ref, move_ref, 0, tiles)):
                lw_ref[s, pl.ds(pl.multiple_of(r * 32, 32), 32), :] = block
            names = place_some(r, names)
        return names

    names_ref[...] = lax.fori_loop(0, blocks // 2, two, jnp.zeros((8, 128), F32), unroll=4)
    copies = []
    for s in range(tiles):
        part = pl.ds(s * 256, 256)
        l_ref[part, :] = jnp.transpose(lw_ref[s])
        copies.append(pltpu.make_async_copy(l_ref.at[part], l_out.at[part], l_sem.at[s]))
        copies[s].start()
    for copy in copies:
        copy.wait()


def run_lefts(deep, wide, me, owner, slot, left, right, aux_of, dest, coeffs):
    blocks, na, cells = coeffs.shape
    tiles = na // 8
    indices = [pltpu.with_memory_space_constraint(x, pltpu.HBM) for x in (owner, slot, left, right, aux_of, dest)]
    return pl.pallas_call(
        functools.partial(lefts_kernel, deep, wide),
        out_shape=(
            pltpu.HBM((tiles * 256, blocks * 32), BF),
            jax.ShapeDtypeStruct((1024,), jnp.int32),
            jax.ShapeDtypeStruct((8, 128), F32),
        ),
        in_specs=[SM] + [HB] * 6 + [VM],
        out_specs=(HB, SM, VM),
        scratch_shapes=[pltpu.SMEM(x.shape, jnp.int32) for x in indices] + [
            pltpu.SemaphoreType.DMA((6,)),
            pltpu.SMEM((PEERS,), jnp.int32),
            pltpu.VMEM((na * 8, 128), F32),
            pltpu.VMEM((na * 8, 128), F32),
            pltpu.VMEM((na * 2, 512), BF),
            pltpu.VMEM((na * 2, 512), BF),
            pltpu.VMEM((512, 512), BF),
            pltpu.VMEM((tiles, blocks * 32, 256), BF),
            pltpu.VMEM((tiles * 256, blocks * 32), BF),
            pltpu.SemaphoreType.DMA((tiles,)),
        ],
        compiler_params=pltpu.CompilerParams(vmem_limit_bytes=16 * MB),
    )(me, *indices, coeffs)


def multiply(coeffs_ref, coulomb_ref, r, y_ref):
    cells = coeffs_ref.shape[2]
    count = coulomb_ref.shape[0] // 8
    for q in range(cells // 256):
        y = jnp.dot(coulomb_ref[...], coeffs_ref[r, :, q * 256:(q + 1) * 256], preferred_element_type=F32)
        put_rows(y_ref, y, q, count)


def turn(y_ref, x_ref, move_ref, w_ref, first, tiles):
    for a in range(y_ref.shape[0] // (64 * tiles)):
        gather_rows(y_ref, x_ref, a * tiles, tiles)
        for s, block in enumerate(turned(x_ref, move_ref, a * tiles, tiles)):
            w_ref[first + a, s * 32:(s + 1) * 32, :] = block


def rights_kernel(begin, end, coeffs_ref, coulomb_ref, after_ref, w_out, y0_ref, y1_ref, x0_ref, x1_ref, move_ref, w_ref, w_sem):
    na = coeffs_ref.shape[1]
    aux = coulomb_ref.shape[0] // na
    tiles = na // 8
    move_ref[...] = lane_move()
    ys, xs = (y0_ref, y1_ref), (x0_ref, x1_ref)
    copies = []
    multiply(coeffs_ref, coulomb_ref, begin, ys[0])
    for r in range(begin, end):
        e = (r - begin) % 2
        if r + 1 < end:
            multiply(coeffs_ref, coulomb_ref, r + 1, ys[1 - e])
        turn(ys[e], xs[e], move_ref, w_ref, (r - begin) * aux, tiles)
        part = pl.ds((r - begin) * aux, aux)
        copies.append(pltpu.make_async_copy(w_ref.at[part], w_out.at[part], w_sem.at[r - begin]))
        copies[-1].start()
    for copy in copies:
        copy.wait()


def rights_scratch(rows):
    return [
        pltpu.VMEM((rows * 8, 128), F32),
        pltpu.VMEM((rows * 8, 128), F32),
        pltpu.VMEM((rows * 2, 512), BF),
        pltpu.VMEM((rows * 2, 512), BF),
        pltpu.VMEM((512, 512), BF),
    ]


def run_rights(coeffs, vall, after, begin, end):
    na = coeffs.shape[1]
    aux = vall.shape[0] // na
    shape = ((end - begin) * aux, na // 8 * 32, 256)
    return pl.pallas_call(
        functools.partial(rights_kernel, begin, end),
        out_shape=pltpu.HBM(shape, BF),
        in_specs=[VM, VM, pl.BlockSpec(memory_space=pl.ANY)],
        out_specs=HB,
        scratch_shapes=rights_scratch(vall.shape[0]) + [
            pltpu.VMEM(shape, BF),
            pltpu.SemaphoreType.DMA((end - begin,)),
        ],
        compiler_params=pltpu.CompilerParams(vmem_limit_bytes=20 * MB),
    )(coeffs, vall, after)


def near_kernel(begin, end, coeffs_ref, coulomb_ref, after_ref, w_ref, y0_ref, y1_ref, x0_ref, x1_ref, move_ref):
    na = coeffs_ref.shape[1]
    aux = coulomb_ref.shape[0] // na
    move_ref[...] = lane_move()
    ys, xs = (y0_ref, y1_ref), (x0_ref, x1_ref)
    multiply(coeffs_ref, coulomb_ref, begin, ys[0])
    for r in range(begin, end):
        e = (r - begin) % 2
        if r + 1 < end:
            multiply(coeffs_ref, coulomb_ref, r + 1, ys[1 - e])
        turn(ys[e], xs[e], move_ref, w_ref, (r - begin) * aux, na // 8)


def run_near(coeffs, vall, after, begin, end):
    na = coeffs.shape[1]
    aux = vall.shape[0] // na
    return pl.pallas_call(
        functools.partial(near_kernel, begin, end),
        out_shape=jax.ShapeDtypeStruct(((end - begin) * aux, na // 8 * 32, 256), BF),
        in_specs=[VM, VM, pl.BlockSpec(memory_space=pl.ANY)],
        out_specs=VM,
        scratch_shapes=rights_scratch(vall.shape[0]),
        compiler_params=pltpu.CompilerParams(vmem_limit_bytes=20 * MB),
    )(coeffs, vall, after)


def tasks_kernel(table_ref, names_ref, coeffs_ref, coulomb_ref, w1_in, w2_in, l_in, d_ref, e_ref,
                 out_ref, y0_ref, y1_ref, x0_ref, x1_ref, move_ref, dl_ref, a_ref, send_ref, w_ref, l_ref, sem):
    tiles = l_ref.shape[0] // 256
    blocks = l_ref.shape[1] // 32
    aux = w_ref.shape[0] // blocks
    tasks = dl_ref.shape[0] // 32
    groups = tasks // 8
    slots = out_ref.shape[1]
    half = d_ref.shape[0]

    here = pl.ds(0, w1_in.shape[0])
    there = pl.ds(w1_in.shape[0], w2_in.shape[0])
    copies = [
        pltpu.make_async_copy(l_in, l_ref, sem.at[0]),
        pltpu.make_async_copy(w1_in, w_ref.at[here], sem.at[1]),
        pltpu.make_async_copy(w2_in, w_ref.at[there], sem.at[2]),
    ]
    for i in (1, 0, 2):
        copies[i].start()
    move_ref[...] = lane_move()
    ys, xs = (y0_ref, y1_ref), (x0_ref, x1_ref)
    begin = (w1_in.shape[0] + w2_in.shape[0]) // aux
    for r in range(begin, blocks):
        multiply(coeffs_ref, coulomb_ref, r, ys[r % 2])
    for r in range(begin, blocks):
        turn(ys[r % 2], xs[r % 2], move_ref, w_ref, r * aux, tiles)
    send_ref[...] = jnp.zeros_like(send_ref)

    spread = ones_where((iota((256, 64), 0) >> 2) == iota((256, 64), 1))
    own_chunk = (iota((256, 128), 0) & 3) == (iota((256, 128), 1) >> 5)
    repeat = ones_where((iota((128, 256), 0) & 31) == (iota((128, 256), 1) & 31))
    for g in range(groups):
        picked = []
        for u in range(8):
            spot = table_ref[g * 8 + u]
            here = lax.rem(spot, half)
            picked.append(jnp.where(spot < half, d_ref[here].astype(F32), e_ref[here].astype(F32)))
        e = jnp.dot(spread, jnp.concatenate(picked, axis=0).astype(BF), preferred_element_type=F32)
        e = jnp.where(own_chunk, e, 0.0).astype(BF)
        dl_ref[g * 256:(g + 1) * 256, :] = jnp.dot(e, repeat, preferred_element_type=F32).astype(BF)

    diag = ones_where((iota((256, 256), 0) >> 5) == (iota((256, 256), 1) >> 5))
    fold = ones_where((iota((256, 128), 0) & 31) == (iota((256, 128), 1) & 31))
    chunk = iota((8, 128), 1) >> 5
    column = iota((32, 256), 1) >> 5

    def apply(g, carry):
        for u in range(64):
            t = g * 64 + u
            rows = pl.ds(pl.multiple_of(t * 32, 32), 32)
            bd = jnp.concatenate([dl_ref[rows, :]] * 8, axis=0) * diag
            y = jnp.dot(w_ref[table_ref[tasks + t]], bd, preferred_element_type=F32).astype(BF)
            for s in range(tiles):
                a_ref[rows, s * 256:(s + 1) * 256] = y[s * 32:(s + 1) * 32, :]
        return carry

    def close(g, carry):
        rows = pl.ds(pl.multiple_of(g * 2048, 2048), 2048)
        total = jnp.dot(a_ref[rows, :], l_ref[...], preferred_element_type=F32)
        own = [jnp.where(column == table_ref[2 * tasks + g * 64 + u], total[u * 32:(u + 1) * 32, :], 0.0) for u in range(64)]
        total = jnp.dot(jnp.concatenate(own, axis=0).astype(BF), fold, preferred_element_type=F32)
        for u in range(64):
            block = total[u * 32:u * 32 + 8, :]
            for q in range(1, 4):
                block = jnp.where(chunk == q, total[u * 32 + q * 8:u * 32 + q * 8 + 8, :], block)
            send_ref[table_ref[3 * tasks + g * 64 + u]] = block
        return carry

    copies[1].wait()
    copies[2].wait()
    lax.fori_loop(0, tasks // 64, apply, 0)
    copies[0].wait()
    lax.fori_loop(0, tasks // 64, close, 0)
    names = names_ref[...]
    for p in range(out_ref.shape[0]):
        send_ref[p * slots + slots - 1] = jnp.broadcast_to(names[p:p + 1, :], (8, 128))
    out_ref[...] = send_ref[...].reshape(out_ref.shape).astype(out_ref.dtype)


def run_tasks(table, names, coeffs, vall, w1, w2, l, dens, other, tasks, peers, cap):
    w1, l = (pltpu.with_memory_space_constraint(x, pltpu.HBM) for x in (w1, l))
    blocks, na, _ = coeffs.shape
    return pl.pallas_call(
        tasks_kernel,
        out_shape=jax.ShapeDtypeStruct((peers, cap + 1, 8, 128), BF),
        in_specs=[SM, VM, VM, VM, HB, pl.BlockSpec(memory_space=pl.ANY), HB, VM, VM],
        out_specs=VM,
        scratch_shapes=rights_scratch(vall.shape[0]) + [
            pltpu.VMEM((tasks * 32, 256), BF),
            pltpu.VMEM((tasks * 32, l.shape[0]), BF),
            pltpu.VMEM((peers * (cap + 1), 8, 128), F32),
            pltpu.VMEM((blocks * (vall.shape[0] // na),) + w1.shape[1:], BF),
            pltpu.VMEM(l.shape, BF),
            pltpu.SemaphoreType.DMA((3,)),
        ],
        compiler_params=pltpu.CompilerParams(vmem_limit_bytes=40 * MB),
    )(table, names, coeffs, vall, w1, w2, l, dens, other)


def spread_kernel(recv_ref, out_ref, flat_ref):
    peers, slots = recv_ref.shape[0], recv_ref.shape[1]
    cap = slots - 1
    rows = out_ref.shape[0]
    names = recv_ref[0, cap].astype(F32)
    for p in range(1, peers):
        names = names + recv_ref[p, cap].astype(F32)
    names = jnp.broadcast_to(names[0:1, :], (rows, 128)).astype(jnp.int32)
    hot = ones_where(iota((rows, 128), 0) + 1 == names)
    for p in range(peers):
        for n in range(cap):
            flat_ref[(p * cap + n) * 8:(p * cap + n + 1) * 8, :] = recv_ref[p, n].astype(F32)
    sums = []
    for i in range(8):
        x = flat_ref[pl.ds(i, 128, stride=8), :]
        sums.append(jnp.dot(hot, x.astype(BF), preferred_element_type=F32))
    for i in range(8):
        flat_ref[pl.ds(i, rows, stride=8), :] = sums[i]
    out_ref[...] = flat_ref[0:rows * 8, :].reshape(rows, 8, 128).astype(out_ref.dtype)


def run_spread(recv, rows, dtype):
    peers, slots = recv.shape[:2]
    return pl.pallas_call(
        spread_kernel,
        out_shape=jax.ShapeDtypeStruct((rows, 8, 128), dtype),
        in_specs=[VM],
        out_specs=VM,
        scratch_shapes=[pltpu.VMEM((max(rows, peers * (slots - 1)) * 8, 128), F32)],
        compiler_params=pltpu.CompilerParams(vmem_limit_bytes=8 * MB),
    )(recv)


def exact_dot(x, y):
    out = None
    for _ in range(3):
        part = x.astype(BF)
        x = x - part.astype(F32)
        term = jnp.dot(part, y, preferred_element_type=F32)
        out = term if out is None else out + term
    return out


def halfway_kernel(recv_ref, out_ref):
    deep = out_ref.shape[0]
    total = recv_ref[0:deep].astype(F32)
    for y in range(1, recv_ref.shape[0] // deep):
        total = total + recv_ref[y * deep:(y + 1) * deep].astype(F32)
    out_ref[...] = total


def run_halfway(recv, wide):
    return pl.pallas_call(
        halfway_kernel,
        out_shape=jax.ShapeDtypeStruct((recv.shape[0] // wide, 8, 128), F32),
        in_specs=[VM],
        out_specs=VM,
        compiler_params=pltpu.CompilerParams(vmem_limit_bytes=4 * MB),
    )(recv)


def final_kernel(recv_ref, out_ref):
    total = jnp.sum(recv_ref[...].astype(F32), axis=0) * -0.25
    vi = iota((64, 128), 0) >> 3
    wide = jnp.concatenate([total] * 8, axis=0)
    wide = jnp.where((iota((64, 128), 1) & 7) == vi, wide, 0.0)
    r, c = iota((128, 128), 0), iota((128, 128), 1)
    move = ones_where((r >> 3) == ((c & 3) << 2) + (c >> 5))
    wide = exact_dot(wide, move)
    wide = jnp.where(((iota((64, 128), 1) >> 2) & 7) == (iota((64, 128), 0) & 7), wide, 0.0)
    out_ref[...] = jnp.sum(wide.reshape(8, 8, 128), axis=1)


def run_final(recv):
    return pl.pallas_call(
        final_kernel,
        out_shape=jax.ShapeDtypeStruct((8, 128), F32),
        in_specs=[VM],
        out_specs=VM,
        compiler_params=pltpu.CompilerParams(vmem_limit_bytes=4 * MB),
    )(recv)


def per_device(coeffs, coulomb, density, task_owner, task_slot, task_left, task_right, task_aux, task_dest):
    na = coeffs.shape[1]
    blk, task = lax.axis_size("x") * lax.axis_size("core"), lax.axis_size("z") * lax.axis_size("y")
    chips = blk // CORES
    dens = lax.all_to_all(run_pack(density, chips), "x", 0, 0, tiled=True)
    me = lax.axis_index(BLK).astype(jnp.int32).reshape(1)
    vall = coulomb.reshape(coulomb.shape[0] * na, na)
    l, table, names = run_lefts(lax.axis_size("z"), lax.axis_size("y"), me, task_owner.reshape(-1), task_slot, task_left, task_right, task_aux, task_dest, coeffs)
    w1 = run_rights(coeffs, vall, names, 0, CUT1)
    dens = dens.reshape(chips * HELD, 8, 128)
    dens, l, table, names, w1 = lax.optimization_barrier((dens, l, table, names, w1))
    other = lax.ppermute(dens, "core", [(0, 1), (1, 0)])
    w2 = run_near(coeffs, vall, dens, CUT1, CUT2)
    send = run_tasks(table, names, coeffs, vall, w1, w2, l, dens, other, task_slot.shape[0], blk, 128 // blk)
    recv = lax.all_to_all(send, BLK, 0, 0, tiled=True)
    rows = run_spread(recv, task, BF)
    back = run_halfway(lax.all_to_all(rows, "y", 0, 0, tiled=True), lax.axis_size("y"))
    back = lax.all_to_all(back, "z", 0, 0, tiled=True)
    return run_final(back).reshape(1, density.shape[1])


BLK = ("x", "core")


def solution(mesh):
    wide = math.gcd(mesh.shape["task"], 8)
    sizes = (mesh.shape["task"] // wide, wide, mesh.shape["blk"] // CORES, CORES)
    fine = jax.sharding.Mesh(mesh.devices.reshape(sizes), ("z", "y", "x", "core"))
    every = P(("z", "y", "x", "core"))
    placed = (every, every, P(BLK), every, every, every, every, every, every)
    return jax.shard_map(per_device, mesh=fine, in_specs=placed, out_specs=every, check_vma=False)
```
